32 devices in a mesh: slab: 16 (over z, y, x), row: 2 (over core).
Axes of the slice: x: 2, y: 2, z: 4, core: 2. Of those that a mesh axis runs over, the one named last changes fastest.
Arguments:
- diag_block: float32 [16, 2, 512, 512], P('slab', None, 'row'), may hold values from -3 to 8
- lower_block: float32 [16, 2, 512, 512], P('slab', None, 'row'), may hold values from -0.4375 to 0.4375
- upper_block: float32 [16, 2, 512, 512], P('slab', None, 'row'), may hold values from -0.4375 to 0.4375
- twist: int32 [16, 512], P('slab'), may hold values from 0 to 511, each once within a row
- excitation: float32 [16, 2, 512, 128], P('slab', None, 'row'), may hold values from -24 to 24
Outputs:
- solution: float32 [16, 2, 512, 128], P('slab', None, 'row')
The draws below stay inside these ranges and needn't reach their ends.
Inputs may be any that keep to these rules, and one draw needn't show every extreme that they name: Each row of twist is a permutation of 0 to 511.
All inputs are finite; a program needn't handle non-finite values.
Results may differ from the reference program's by a relative error of at most 0.00014.
Values sent between devices are 32-bit elements; how exact they have to be, the bound alone decides.
No kernel may reach another device: no remote copies, remote signals or barrier semaphores. Data moves between devices by JAX's collectives and lax.ppermute only.
A program may use at most 128 MiB of HBM per device.

```python
import jax
import jax.numpy as jnp
from jax import lax

STRANDS = 512
PATTERNS = 128
NS_STEPS = 3
SLABS = 16


def draw_diag_block(key, part):
    noise_key, resist_key, react_key = jax.random.split(key, 3)
    shape = (SLABS, 2, STRANDS, STRANDS)
    noise = jnp.clip(jax.random.normal(noise_key, shape, jnp.float32), -6.0, 6.0)
    noise = noise * (1.0 / jnp.sqrt(jnp.float32(STRANDS)))
    resist = jax.random.uniform(resist_key, (SLABS, STRANDS), jnp.float32, 4.0, 6.0)
    react = jax.random.uniform(react_key, (SLABS, STRANDS), jnp.float32, -1.0, 1.0)
    identity = (lax.broadcasted_iota(jnp.int32, (STRANDS, STRANDS), 0) == lax.broadcasted_iota(jnp.int32, (STRANDS, STRANDS), 1)).astype(jnp.float32)
    diagonal_part = jnp.stack([resist[:, :, None] * identity, react[:, :, None] * identity], axis=1)
    return noise + diagonal_part


def levels(rng, extent, pieces, low, high):
    factor_of = 1.0
    for position, shards_of in pieces:
        steps = jax.random.uniform(jax.random.fold_in(jax.random.fold_in(rng, 6), position), (shards_of,), jnp.float32, low / len(pieces), high / len(pieces))
        factor_of = factor_of * jnp.repeat(jnp.exp(steps), extent[position] // shards_of).reshape((-1,) + (1,) * (len(extent) - 1 - position))
    return factor_of


def centred(key, dims, deviation, reach, shards=(), held_as=jnp.bfloat16):
    result = deviation * jax.random.normal(key, dims, jnp.float32)
    if shards:
        result = result * levels(key, dims, shards, -0.22, 0.18)
    return jnp.clip(result, -reach, reach).astype(held_as)


def setup_inputs(seed: int = 0) -> dict:
    splits = jax.random.split(jax.random.key(seed), 6)
    diag_block = draw_diag_block(jax.random.fold_in(splits[5], 71), 0)
    lower_block = centred(splits[1], (SLABS, 2, STRANDS, STRANDS), (STRANDS // 3) ** -0.5, 0.4375, ((0, 16), (2, 2)), jnp.float32)
    upper_block = centred(splits[2], (SLABS, 2, STRANDS, STRANDS), (STRANDS // 3) ** -0.5, 0.4375, ((0, 16), (2, 2)), jnp.float32)
    twist = jax.vmap(lambda own: jax.random.permutation(own, STRANDS))(jax.random.split(splits[3], SLABS)).reshape((SLABS, STRANDS)).astype(jnp.int32)
    excitation = centred(splits[4], (SLABS, 2, STRANDS, PATTERNS), 4.0, 24.0, ((0, 16), (2, 2)), jnp.float32)
    return {"diag_block": diag_block, "lower_block": lower_block, "upper_block": upper_block, "twist": twist, "excitation": excitation}


def complex_product(left_mat, right_mat):
    exact = lax.Precision.HIGHEST
    real_part = jnp.matmul(left_mat[..., 0, :, :], right_mat[..., 0, :, :], precision=exact) - jnp.matmul(left_mat[..., 1, :, :], right_mat[..., 1, :, :], precision=exact)
    imag_part = jnp.matmul(left_mat[..., 0, :, :], right_mat[..., 1, :, :], precision=exact) + jnp.matmul(left_mat[..., 1, :, :], right_mat[..., 0, :, :], precision=exact)
    return jnp.stack([real_part, imag_part], axis=-3)


def newton_inverse(blocks):
    identity = jnp.eye(blocks.shape[-1], dtype=blocks.dtype)
    iterate = jnp.stack([0.4 * identity - 0.04 * blocks[:, 0], -0.04 * blocks[:, 1]], axis=1)
    for iteration in range(NS_STEPS - 1):
        iterate = 2.0 * iterate - complex_product(complex_product(iterate, blocks), iterate)
    return iterate


def twist_columns(block, strand_order):
    return jnp.take(block, strand_order, axis=2)


def reference(diag_block, lower_block, upper_block, twist, excitation):
    slab_ids = jnp.arange(SLABS)
    lower_twisted = jax.vmap(twist_columns)(lower_block, twist) * (slab_ids > 0).astype(lower_block.dtype)[:, None, None, None]
    upper_twisted = jax.vmap(twist_columns)(upper_block, twist) * (slab_ids < SLABS - 1).astype(upper_block.dtype)[:, None, None, None]
    lower_odd = lower_twisted[1::2]
    upper_odd = upper_twisted[1::2]
    drive_odd = excitation[1::2]
    first_inverse = newton_inverse(diag_block[1::2])
    from_below = complex_product(lower_twisted[0::2], jnp.roll(first_inverse, 1, axis=0))
    from_above = complex_product(upper_twisted[0::2], first_inverse)
    diag_one = diag_block[0::2] - complex_product(from_below, jnp.roll(upper_odd, 1, axis=0)) - complex_product(from_above, lower_odd)
    lower_one = -complex_product(from_below, jnp.roll(lower_odd, 1, axis=0))
    upper_one = -complex_product(from_above, upper_odd)
    drive_one = excitation[0::2] - complex_product(from_below, jnp.roll(drive_odd, 1, axis=0)) - complex_product(from_above, drive_odd)
    second_inverse = newton_inverse(diag_one[1::2])
    below_two = complex_product(lower_one[0::2], jnp.roll(second_inverse, 1, axis=0))
    above_two = complex_product(upper_one[0::2], second_inverse)
    diag_two = diag_one[0::2] - complex_product(below_two, jnp.roll(upper_one[1::2], 1, axis=0)) - complex_product(above_two, lower_one[1::2])
    drive_two = drive_one[0::2] - complex_product(below_two, jnp.roll(drive_one[1::2], 1, axis=0)) - complex_product(above_two, drive_one[1::2])
    coarse_solution = complex_product(newton_inverse(diag_two), drive_two)
    residual_two = drive_one[1::2] - complex_product(lower_one[1::2], coarse_solution) - complex_product(upper_one[1::2], jnp.roll(coarse_solution, -1, axis=0))
    middle_solution = complex_product(second_inverse, residual_two)
    even_solution = jnp.stack([coarse_solution, middle_solution], axis=1).reshape((SLABS // 2,) + excitation.shape[1:])
    residual_one = drive_odd - complex_product(lower_odd, even_solution) - complex_product(upper_odd, jnp.roll(even_solution, -1, axis=0))
    odd_solution = complex_product(first_inverse, residual_one)
    return jnp.stack([even_solution, odd_solution], axis=1).reshape(excitation.shape)
```

```python
import functools

import jax
import jax.numpy as jnp
from jax import lax
from jax.experimental import pallas as pl
from jax.experimental.pallas import tpu as pltpu
from jax.sharding import PartitionSpec as P

F32 = jnp.float32
BF16 = jnp.bfloat16
TILE = 256


def halves(x):
    high = x.astype(BF16)
    return high, (x - high.astype(F32)).astype(BF16)


def put(high, low, rows, cols, real, imag):
    for part, value in enumerate((real, imag, real + imag)):
        h, l = halves(value)
        high[part, rows, cols] = h
        low[part, rows, cols] = l


def dot(a, b):
    return jnp.dot(a, b, preferred_element_type=F32)


def product(ah, al, bh, bl, cols, rows=slice(None)):
    terms = []
    for part in range(3):
        xh, xl = ah[part, rows, :], al[part, rows, :]
        yh, yl = bh[part, :, cols], bl[part, :, cols]
        terms.append(dot(xh, yh) + dot(xh, yl) + dot(xl, yh))
    first, second, third = terms
    return first - second, third - first - second


def apply(ah, al, real, imag, rows=slice(None)):
    width = real.shape[1]
    vh, vl = halves(jnp.concatenate([real, imag], axis=1))
    sides = []
    for part in range(2):
        xh, xl = ah[part, rows, :], al[part, rows, :]
        sides.append(dot(xh, vh) + dot(xh, vl) + dot(xl, vh))
    first, second = sides
    return (
        first[:, :width] - second[:, width:],
        first[:, width:] + second[:, :width],
    )


def eye(rows, cols, row_start, col_start):
    return (
        lax.broadcasted_iota(jnp.int32, (rows, cols), 0) + row_start
        == lax.broadcasted_iota(jnp.int32, (rows, cols), 1) + col_start
    ).astype(F32)


def tiles(width, start=0):
    def run(step):
        if width % TILE:
            for begin in range(0, width, 128):
                step(pl.ds(start + begin, 128), begin)
            return

        @pl.loop(0, width // TILE)
        def _(index):
            begin = pl.multiple_of(index * TILE, TILE)
            step(pl.ds(pl.multiple_of(start + begin, 128), TILE), begin)

    return run


def twist_kernel(info, lower, upper, order, drive, diag, first, second, joined, coarse):
    strands = lower.shape[2]
    pick = (
        lax.broadcasted_iota(jnp.int32, (strands, strands), 0) == order[...]
    ).astype(BF16)
    is_a = info[1] == 1
    width = drive.shape[2]
    for part in range(2):
        moved = []
        for source in (lower, upper):
            value = source[part]
            high, rest = halves(value)
            middle, low = halves(value - high.astype(F32))
            moved.append(dot(high, pick) + dot(middle, pick) + dot(low, pick))
        one = jnp.where(is_a, moved[1], moved[0])
        two = jnp.where(is_a, moved[0], moved[1])
        first[part] = one
        second[part] = two
        joined[part, :, :strands] = one
        joined[part, :, strands : strands + width] = drive[part]
        joined[part, :, strands + width :] = two
        coarse[part, :, :strands] = diag[part]
        coarse[part, :, strands:] = drive[part]


def load_step(info, own, other, mf, mh, ml):
    count = own.shape[1]
    strands = mf.shape[2]
    here = pl.multiple_of(info[0] * count, count)
    there = pl.multiple_of((1 - info[0]) * count, count)
    for start, source in ((here, own), (there, other)):
        rows = pl.ds(start, count)
        real = eye(count, strands, start, 0) - 0.2 * source[0, :, :strands]
        imag = -0.2 * source[1, :, :strands]
        mf[0, rows, :] = real
        mf[1, rows, :] = imag
        put(mh, ml, rows, slice(None), real, imag)


def square(mh, ml, nf, nh, nl):
    @tiles(mh.shape[2])
    def _(cols, begin):
        real, imag = product(mh, ml, mh, ml, cols)
        if nf is not None:
            nf[0, :, cols] = real
            nf[1, :, cols] = imag
        put(nh, nl, slice(None), cols, real, imag)


def inverse(mf, mh, ml, nf, nh, nl, qh, ql, fh, fl, finish):
    strands = mh.shape[2]

    @tiles(strands)
    def _(cols, begin):
        real, imag = product(mh, ml, nh, nl, cols)
        real = real + mf[0, :, cols] + nf[0, :, cols] + eye(strands, TILE, 0, begin)
        imag = imag + mf[1, :, cols] + nf[1, :, cols]
        mf[0, :, cols] = real
        mf[1, :, cols] = imag
        put(qh, ql, slice(None), cols, real, imag)

    square(nh, nl, None, fh, fl)

    @tiles(strands)
    def _(cols, begin):
        real, imag = product(fh, fl, qh, ql, cols)
        finish(cols, 0.2 * (real + mf[0, :, cols]), 0.2 * (imag + mf[1, :, cols]))


def first_kernel(
    info, own, other, wide_own, wide_other, reh, rel,
    mf, mh, ml, nf, nh, nl, qh, ql, fh, fl, wh, wl,
):
    load_step(info, own, other, mf, mh, ml)
    count = own.shape[1]
    strands = mh.shape[2]
    here = pl.multiple_of(info[0] * count, count)
    there = pl.multiple_of((1 - info[0]) * count, count)
    for start, source in ((here, wide_own), (there, wide_other)):
        put(wh, wl, pl.ds(start, count), slice(None), source[0], source[1])
    square(mh, ml, nf, nh, nl)

    def finish(cols, real, imag):
        put(mh, ml, slice(None), cols, real, imag)

    inverse(mf, mh, ml, nf, nh, nl, qh, ql, fh, fl, finish)
    width = wh.shape[2] - 2 * strands

    def spread(cols, begin):
        real, imag = product(mh, ml, wh, wl, cols)
        put(reh, rel, slice(None), cols, real, imag)

    tiles(strands)(spread)
    tiles(width, strands)(spread)
    tiles(strands, strands + width)(spread)


def couple_kernel(begin_col, info, one, two, reh, rel, out, ch, cl):
    swap = info[1] == 1
    real = jnp.where(swap, one[0], two[0])
    imag = jnp.where(swap, one[1], two[1])
    put(ch, cl, slice(None), slice(None), real, imag)

    def step(cols, begin):
        real, imag = product(ch, cl, reh, rel, cols)
        place = pl.ds(begin, cols.size)
        out[0, :, place] = real
        out[1, :, place] = imag

    total = out.shape[2]
    whole = total // TILE * TILE
    done = 0
    for width in (whole, total - whole):
        if width:
            def shifted(cols, begin, done=done):
                step(cols, begin + done)

            tiles(width, begin_col + done)(shifted)
            done += width


def step_right(source, gh, gl, bh, bl, target, base):
    put(gh, gl, slice(None), slice(None), source[0], source[1])

    @tiles(target.shape[2])
    def _(cols, begin):
        real, imag = product(gh, gl, bh, bl, cols)
        if base is not None:
            real = real + base[0, :, cols]
            imag = imag + base[1, :, cols]
        target[0, :, cols] = real
        target[1, :, cols] = imag


def second_kernel(
    info, own, other, kc_own, kc_other, far, base, out, mf, mh, ml, nh, nl, kch, kcl,
    g, k, gh, gl, bh, bl,
):
    load_step(info, own, other, mf, mh, ml)
    count = own.shape[1]
    strands = mh.shape[2]
    width = own.shape[2] - strands
    here = pl.multiple_of(info[0] * count, count)
    there = pl.multiple_of((1 - info[0]) * count, count)
    every = slice(None)
    for start, source, side in ((here, kc_own, own), (there, kc_other, other)):
        rows = pl.ds(start, count)
        put(kch, kcl, rows, every, source[0], source[1])
        put(bh, bl, rows, every, side[0, :, strands:], side[1, :, strands:])
    square(mh, ml, None, nh, nl)
    g[...] = far[:, :, :strands]
    step_right(g, gh, gl, mh, ml, k, g)
    step_right(k, gh, gl, nh, nl, g, k)
    step_right(g, gh, gl, nh, nl, k, None)
    step_right(k, gh, gl, nh, nl, k, g)
    put(gh, gl, every, every, 0.2 * k[0], 0.2 * k[1])

    @tiles(strands)
    def _(cols, begin):
        real, imag = product(gh, gl, kch, kcl, cols)
        source = pl.ds(pl.multiple_of(strands + width + begin, 128), TILE)
        out[0, :, cols] = base[0, :, cols] - far[0, :, source] - real
        out[1, :, cols] = base[1, :, cols] - far[1, :, source] - imag

    real, imag = product(gh, gl, bh, bl, every)
    side = pl.ds(strands, width)
    out[0, :, side] = base[0, :, side] - far[0, :, side] + real
    out[1, :, side] = base[1, :, side] - far[1, :, side] + imag


def shadow_kernel(
    info, mf, mh, ml, nh, nl, reh, rel, zh, zl, pf, qh, ql, fh, fl, yh, yl,
):
    count = zh.shape[1] // 2
    strands = mh.shape[2]
    here = pl.ds(pl.multiple_of(info[0] * count, count), count)
    every = slice(None)

    @tiles(strands)
    def _(cols, begin):
        real, imag = product(mh, ml, nh, nl, cols)
        square_real = nh[0, :, cols].astype(F32) + nl[0, :, cols].astype(F32)
        square_imag = nh[1, :, cols].astype(F32) + nl[1, :, cols].astype(F32)
        real = real + mf[0, :, cols] + square_real + eye(strands, TILE, 0, begin)
        imag = imag + mf[1, :, cols] + square_imag
        pf[0, :, cols] = real
        pf[1, :, cols] = imag
        put(qh, ql, every, cols, real, imag)

    square(nh, nl, None, fh, fl)

    @tiles(strands)
    def _(cols, begin):
        real, imag = product(fh, fl, qh, ql, cols)
        put(
            yh, yl, every, cols,
            0.2 * (real + pf[0, :, cols]), 0.2 * (imag + pf[1, :, cols]),
        )

    zh[:, :count, :] = yh[:, here, :]
    zl[:, :count, :] = yl[:, here, :]

    @tiles(strands)
    def _(cols, begin):
        real, imag = product(
            reh.at[:, :, pl.ds(0, strands)], rel.at[:, :, pl.ds(0, strands)],
            yh, yl, cols, here,
        )
        put(zh, zl, pl.ds(count, count), cols, real, imag)


def coarse_kernel(info, own, other, kch, kcl, fine, xh, xl, xr, vr, mf, mh, ml, bf):
    load_step(info, own, other, mf, mh, ml)
    count = own.shape[1]
    strands = mh.shape[2]
    here = pl.multiple_of(info[0] * count, count)
    there = pl.multiple_of((1 - info[0]) * count, count)
    for start, source in ((here, own), (there, other)):
        bf[:, pl.ds(start, count), :] = source[:, :, strands:]
    real, imag = bf[0], bf[1]
    for _ in range(7):
        real, imag = apply(mh, ml, real, imag)
        real = bf[0] + real
        imag = bf[1] + imag
    real = 0.2 * real
    imag = 0.2 * imag
    rows = pl.ds(here, count)
    bf[0] = real
    bf[1] = imag
    xr[...] = bf[:, rows, :]
    high, low = halves(jnp.concatenate([real, imag], axis=1))
    xh[...] = high
    xl[...] = low
    real, imag = apply(kch, kcl, real, imag, rows)
    vr[0] = fine[0, :, strands:] + real
    vr[1] = fine[1, :, strands:] + imag
    vr[2] = real
    vr[3] = imag


def apply_held(ah, al, vh, vl, rows, cols):
    width = vh.shape[1] // 2
    sides = []
    for part in range(2):
        a, b = ah[part, rows, cols], al[part, rows, cols]
        sides.append(dot(a, vh[...]) + dot(a, vl[...]) + dot(b, vh[...]))
    first, second = sides
    return (
        first[:, :width] - second[:, width:],
        first[:, width:] + second[:, :width],
    )


def last_kernel(info, own, other, zh, zl, reh, rel, xh, xl, middle, odd, vf):
    count = own.shape[1]
    strands = zh.shape[2]
    width = own.shape[2]
    here = pl.multiple_of(info[0] * count, count)
    there = pl.multiple_of((1 - info[0]) * count, count)
    for start, source in ((here, own), (there, other)):
        vf[:, pl.ds(start, count), :] = source[...]
    real, imag = apply(zh, zl, vf[0], vf[1])
    middle[0] = real[:count]
    middle[1] = imag[:count]
    rows = pl.ds(here, count)
    side = pl.ds(strands, width)
    tail = pl.ds(strands + width, strands)
    far_real, far_imag = apply_held(reh, rel, xh, xl, rows, tail)
    near = [
        reh[part, rows, side].astype(F32) + rel[part, rows, side].astype(F32)
        for part in range(2)
    ]
    odd[0] = near[0] - far_real - real[count:]
    odd[1] = near[1] - far_imag - imag[count:]


VMEM = pl.BlockSpec(memory_space=pltpu.VMEM)
SMEM = pl.BlockSpec(memory_space=pltpu.SMEM)


def call(kernel, info, arrays, outs, scratch, flops):
    shapes = [jax.ShapeDtypeStruct(shape, dtype) for shape, dtype in outs]
    moved = sum(x.size * x.dtype.itemsize for x in list(arrays) + shapes)
    return pl.pallas_call(
        kernel,
        out_shape=shapes,
        in_specs=[SMEM] + [VMEM] * len(arrays),
        out_specs=[VMEM] * len(outs),
        scratch_shapes=[pltpu.VMEM(shape, dtype) for shape, dtype in scratch],
        compiler_params=pltpu.CompilerParams(vmem_limit_bytes=58 * 2**20),
        cost_estimate=pl.CostEstimate(
            flops=int(flops), bytes_accessed=int(moved), transcendentals=0
        ),
    )(info, *arrays)


def body(diag_block, lower_block, upper_block, twist, excitation):
    slabs = lax.axis_size("slab")
    slab = lax.axis_index("slab")
    row = lax.axis_index("row")
    diag, lower, upper, drive = diag_block[0], lower_block[0], upper_block[0], excitation[0]
    count, strands = diag.shape[1:]
    width = drive.shape[2]
    narrow = strands + width
    wide = strands + narrow
    info = jnp.stack([row, (slab % 4 == 1).astype(row.dtype)]).astype(jnp.int32)
    unit = 18 * strands**3

    def pairs(phase, by):
        return [
            (i, i + by) for i in range(slabs) if i % 4 == phase and 0 <= i + by < slabs
        ]

    def send(x, *moves):
        return lax.ppermute(x, "slab", [pair for move in moves for pair in pairs(*move)])

    def cross(x):
        return lax.ppermute(x, "row", [(0, 1), (1, 0)])

    def after(x, *gates):
        return lax.optimization_barrier((x,) + gates)[0]

    part = (2, count, strands)
    full = (2, strands, strands)
    trio = (3, strands, strands)
    half = (3, count, strands)
    diag_other = cross(diag)
    first, second, joined, coarse = call(
        twist_kernel, info, [lower, upper, twist, drive, diag],
        [(part, F32), (part, F32), ((2, count, wide), F32), ((2, count, narrow), F32)],
        [], unit / 3,
    )
    near_a = send(first, (2, -1))
    near_b = send(second, (2, 1))
    joined_other = cross(joined)
    reh, rel = call(
        first_kernel, info, [diag, diag_other, joined, joined_other],
        [((3, strands, wide), BF16)] * 2,
        [(full, F32), (trio, BF16), (trio, BF16)] * 2
        + [(trio, BF16)] * 4 + [((3, strands, wide), BF16)] * 2,
        unit * 6.25,
    )
    base_near_a = send(coarse, (2, -1))
    base_near_b = send(coarse, (2, 1))
    second_gate = after(second, reh)
    far_a = send(second_gate, (0, 1))
    far_b = send(after(first, reh), (0, -1))
    base_far = send(after(coarse, far_a), (0, 1))
    pieces = [(half, BF16)] * 2
    (sent,) = call(
        functools.partial(couple_kernel, 0), info, [near_a, near_b, reh, rel],
        [((2, count, narrow), F32)], pieces, unit * 0.625,
    )
    got = send(sent, (1, 2), (3, -2))
    (keep,) = call(
        functools.partial(couple_kernel, narrow), info, [near_a, near_b, reh, rel],
        [(part, F32)], pieces, unit * 0.5,
    )
    keep_other = cross(keep)
    (far,) = call(
        functools.partial(couple_kernel, 0), info, [far_a, far_b, reh, rel],
        [((2, count, wide), F32)], pieces, unit * 1.125,
    )
    fine = base_near_a + base_near_b - sent - got
    fine_other = cross(fine)
    out, mf, mh, ml, nh, nl, kch, kcl = call(
        second_kernel, info,
        [fine, fine_other, keep, keep_other, far, base_far],
        [((2, count, narrow), F32), (full, F32)] + [(trio, BF16)] * 6,
        [(part, F32)] * 2 + pieces + [((3, strands, width), BF16)] * 2,
        unit * 3.625,
    )
    out_got = send(out, (3, 2), (1, -2))
    zh, zl = call(
        shadow_kernel, info, [mf, mh, ml, nh, nl, reh, rel],
        [(trio, BF16)] * 2, [(full, F32)] + [(trio, BF16)] * 6, unit * 3.5,
    )
    total = out + out_got
    total_other = cross(total)
    xh, xl, xr, vr = call(
        coarse_kernel, info, [total, total_other, kch, kcl, fine],
        [((strands, 2 * width), BF16)] * 2
        + [((2, count, width), F32), ((4, count, width), F32)],
        [(full, F32), (trio, BF16), (trio, BF16), ((2, strands, width), F32)],
        unit * 2.5,
    )
    v_got = send(vr[2:], (1, 2), (3, -2))
    x_even = send(xr, (1, -1))
    v = vr[:2] + v_got
    v_other = cross(v)
    middle, odd = call(
        last_kernel, info, [v, v_other, zh, zl, reh, rel, xh, xl],
        [((2, count, width), F32)] * 2, [((2, strands, width), F32)], unit * 0.5,
    )
    x_middle = send(middle, (3, -1))
    return jnp.where(slab % 2 == 1, odd, x_even + x_middle)[None]


def solution(mesh):
    return jax.shard_map(
        body,
        mesh=mesh,
        in_specs=(
            P("slab", None, "row", None),
            P("slab", None, "row", None),
            P("slab", None, "row", None),
            P("slab", None),
            P("slab", None, "row", None),
        ),
        out_specs=P("slab", None, "row", None),
        check_vma=False,
    )
```

```python
import jax
import jax.numpy as jnp
from jax import lax
from jax.experimental import pallas as pl
from jax.experimental.pallas import tpu as pltpu
from jax.sharding import PartitionSpec as P

F32 = jnp.float32
BF16 = jnp.bfloat16
ALL = slice(None)
CHUNKS = 4
TILE = 256


def halves(x):
    high = x.astype(BF16)
    return high, (x - high.astype(F32)).astype(BF16)


def dot(a, b):
    return jnp.dot(a, b, preferred_element_type=F32)


def put_left(ref, rows, real, imag, start=0):
    depth = ref.shape[2] // 3
    count = real.shape[1]
    spans = [pl.ds(pl.multiple_of(block * depth + start, 128), count) for block in range(3)]
    for part, value in enumerate((real, imag, real + imag)[: ref.shape[0]]):
        high, low = halves(value)
        ref[part, rows, spans[0]] = high
        ref[part, rows, spans[1]] = low
        ref[part, rows, spans[2]] = high


def put_right(ref, start, cols, real, imag):
    depth = ref.shape[1] // 3
    count = real.shape[0]
    spans = [pl.ds(pl.multiple_of(block * depth + start, 128), count) for block in range(3)]
    for part, value in enumerate((real, imag, real + imag)):
        high, low = halves(value)
        ref[part, spans[0], cols] = high
        ref[part, spans[1], cols] = high
        ref[part, spans[2], cols] = low


def product(left, right, emit, start=0, width=None, rows=ALL):
    width = right.shape[2] if width is None else width

    def step(begin, extent):
        cols = pl.ds(pl.multiple_of(start + begin, 128), extent)
        first = dot(left[0, rows, :], right[0, :, cols])
        second = dot(left[1, rows, :], right[1, :, cols])
        third = dot(left[2, rows, :], right[2, :, cols])
        emit(begin, pl.ds(begin, extent), first - second, third - first - second)

    whole = width // TILE
    if whole:

        @pl.loop(0, whole)
        def _(index):
            step(pl.multiple_of(index * TILE, TILE), TILE)

    if width % TILE:
        step(whole * TILE, width % TILE)


def fill(target):
    def emit(begin, cols, real, imag):
        target[0, :, cols] = real
        target[1, :, cols] = imag

    return emit


def apply(left, real, imag, rows=ALL):
    width = real.shape[1]
    high, low = halves(jnp.concatenate([real, imag], axis=1))
    stacked = jnp.concatenate([high, high, low], axis=0)
    first = dot(left[0, rows, :], stacked)
    second = dot(left[1, rows, :], stacked)
    return (
        first[:, :width] - second[:, width:],
        first[:, width:] + second[:, :width],
    )


def eye(rows, cols, row_start, col_start=0):
    return (
        lax.broadcasted_iota(jnp.int32, (rows, cols), 0) + row_start
        == lax.broadcasted_iota(jnp.int32, (rows, cols), 1) + col_start
    ).astype(F32)


def places(info, count):
    return (
        pl.multiple_of(info[0] * count, count),
        pl.multiple_of((1 - info[0]) * count, count),
    )


def twist_kernel(info, order, lower, upper, drive, diag, first, second, joined, coarse, pick):
    strands = lower.shape[2]
    width = drive.shape[2]
    rows = lower.shape[1]

    @pl.when(pl.program_id(0) == 0)
    def _():
        pick[...] = (
            lax.broadcasted_iota(jnp.int32, (strands, strands), 0) == order[...]
        ).astype(BF16)

    value = jnp.concatenate([lower[0], lower[1], upper[0], upper[1]], axis=0)
    high, rest = halves(value)
    middle, low = halves(value - high.astype(F32))
    moved = dot(jnp.concatenate([high, middle, low], axis=0), pick[...])
    span = 4 * rows
    moved = (moved[:span] + moved[span : 2 * span]) + moved[2 * span :]
    is_a = info[1] == 1
    for part in range(2):
        down = moved[part * rows : (part + 1) * rows]
        up = moved[(2 + part) * rows : (3 + part) * rows]
        one = jnp.where(is_a, up, down)
        two = jnp.where(is_a, down, up)
        first[part] = one
        second[part] = two
        joined[part, :, :strands] = one
        joined[part, :, strands : strands + width] = drive[part]
        joined[part, :, strands + width :] = two
        coarse[part, :, :strands] = diag[part]
        coarse[part, :, strands:] = drive[part]


def load_step(info, own, other, mf, left, right):
    count = own.shape[1]
    strands = own.shape[1] * 2
    for start, source in zip(places(info, count), (own, other)):
        rows = pl.ds(start, count)
        real = eye(count, strands, start) - 0.2 * source[0, :, :strands]
        imag = -0.2 * source[1, :, :strands]
        if mf is not None:
            mf[0, rows, :] = real
            mf[1, rows, :] = imag
        put_left(left, rows, real, imag)
        if right is not None:
            put_right(right, start, ALL, real, imag)


def square(ml, mr, nf, nl, nr):
    def emit(begin, cols, real, imag):
        nf[0, :, cols] = real
        nf[1, :, cols] = imag
        if nl is not None:
            put_left(nl, ALL, real, imag, begin)
        put_right(nr, 0, cols, real, imag)

    product(ml, mr, emit)


def inverse_tail(mf, ml, mr, nf, nl, nr, finish):
    strands = mf.shape[1]

    def quarter(begin, cols, real, imag):
        mf[0, :, cols] = (
            mf[0, :, cols] + nf[0, :, cols] + real + eye(strands, real.shape[1], 0, begin)
        )
        mf[1, :, cols] = mf[1, :, cols] + nf[1, :, cols] + imag
        put_right(mr, 0, cols, mf[0, :, cols], mf[1, :, cols])

    product(ml, nr, quarter)

    def fourth(begin, cols, real, imag):
        put_left(ml, ALL, real, imag, begin)

    product(nl, nr, fourth)

    def last(begin, cols, real, imag):
        finish(
            begin, cols, 0.2 * (mf[0, :, cols] + real), 0.2 * (mf[1, :, cols] + imag)
        )

    product(ml, mr, last)


def first_kernel(
    info, own, other, wide_own, wide_other, near, far, mf, ml, mr, nf, nl, nr, wr
):
    load_step(info, own, other, mf, ml, mr)
    count = own.shape[1]
    strands = mf.shape[1]
    for start, source in zip(places(info, count), (wide_own, wide_other)):
        put_right(wr, start, ALL, source[0], source[1])
    square(ml, mr, nf, nl, nr)

    def finish(begin, cols, real, imag):
        put_left(nl, ALL, real, imag, begin)

    inverse_tail(mf, ml, mr, nf, nl, nr, finish)
    narrow = near.shape[2]
    product(nl, wr, fill(near), 0, narrow)
    product(nl, wr, fill(far), narrow, strands)


def couple_kernel(info, one, two, right, out, cl, rr):
    swap = info[1] == 1
    put_left(cl, ALL, jnp.where(swap, one[0], two[0]), jnp.where(swap, one[1], two[1]))
    put_right(rr, 0, ALL, right[0], right[1])
    product(cl, rr, fill(out))


def outer_kernel(info, one, two, near, far, near_out, far_out, cl, nr, fr):
    swap = info[1] == 1
    put_left(cl, ALL, jnp.where(swap, one[0], two[0]), jnp.where(swap, one[1], two[1]))
    put_right(nr, 0, ALL, near[0], near[1])
    put_right(fr, 0, ALL, far[0], far[1])
    product(cl, nr, fill(near_out))
    product(cl, fr, fill(far_out))


def step_right(source, gl, right, target, base):
    put_left(gl, ALL, source[0], source[1])

    def emit(begin, cols, real, imag):
        target[0, :, cols] = real if base is None else base[0, :, cols] + real
        target[1, :, cols] = imag if base is None else base[1, :, cols] + imag

    product(gl, right, emit)


def second_kernel(
    info, own, other, kc_own, kc_other, far_near, far_far, out, mf, nf,
    ml, mr, nr, gl, kr, er, g, k,
):
    load_step(info, own, other, mf, ml, mr)
    count = own.shape[1]
    strands = mf.shape[1]
    side = pl.ds(strands, own.shape[2] - strands)
    for start, source, edge in zip(places(info, count), (kc_own, kc_other), (own, other)):
        put_right(kr, start, ALL, source[0], source[1])
        put_right(er, start, ALL, edge[0, :, side], edge[1, :, side])
    square(ml, mr, nf, None, nr)
    g[...] = far_near[:, :, :strands]
    step_right(g, gl, mr, k, g)
    step_right(k, gl, nr, g, k)
    step_right(g, gl, nr, k, None)
    step_right(k, gl, nr, k, g)
    put_left(gl, ALL, 0.2 * k[0], 0.2 * k[1])

    def lower(begin, cols, real, imag):
        out[0, :, cols] = -far_far[0, :, cols] - real
        out[1, :, cols] = -far_far[1, :, cols] - imag

    product(gl, kr, lower)

    def right(begin, cols, real, imag):
        out[0, :, side] = real - far_near[0, :, side]
        out[1, :, side] = imag - far_near[1, :, side]

    product(gl, er, right)


def shadow_kernel(info, mf, nf, near, zr, pf, ml, mr, nl, nr):
    count = zr.shape[1] // 2
    strands = mf.shape[1]
    rows = pl.ds(places(info, count)[0], count)
    head = pl.ds(0, strands)
    pf[...] = mf[...]
    put_left(ml, ALL, mf[0], mf[1])
    put_left(nl, ALL, nf[0], nf[1])
    put_right(nr, 0, ALL, nf[0], nf[1])

    def finish(begin, cols, real, imag):
        pf[0, :, cols] = real
        pf[1, :, cols] = imag

    inverse_tail(pf, ml, mr, nf, nl, nr, finish)
    zr[:, :count, :] = pf[:, rows, :]
    put_right(mr, 0, ALL, pf[0], pf[1])
    top = pl.ds(0, count)
    put_left(nl, top, near[0, rows, head], near[1, rows, head])

    def emit(begin, cols, real, imag):
        zr[0, count:, cols] = real
        zr[1, count:, cols] = imag

    product(nl, mr, emit, rows=top)


def coarse_kernel(info, own, other, keep, fine, xf, xr, wr, vr, ml, kl):
    load_step(info, own, other, None, ml, None)
    count = own.shape[1]
    strands = keep.shape[2]
    for start, source in zip(places(info, count), (own, other)):
        xf[:, pl.ds(start, count), :] = source[:, :, strands:]
    put_left(kl, ALL, keep[0], keep[1])
    real, imag = xf[0], xf[1]
    for _ in range(7):
        real, imag = apply(ml, real, imag)
        real = xf[0] + real
        imag = xf[1] + imag
    real = 0.2 * real
    imag = 0.2 * imag
    xf[0] = real
    xf[1] = imag
    xr[...] = xf[:, pl.ds(places(info, count)[0], count), :]
    real, imag = apply(kl, real, imag)
    wr[0] = real
    wr[1] = imag
    vr[0] = fine[0, :, strands:] + real
    vr[1] = fine[1, :, strands:] + imag


def side_kernel(info, near, far, xf, odd, fl):
    count = odd.shape[1]
    strands = far.shape[2]
    rows = pl.ds(places(info, count)[0], count)
    put_left(fl, ALL, far[0, rows, :], far[1, rows, :])
    real, imag = apply(fl, xf[0], xf[1])
    odd[0] = near[0, rows, strands:] - real
    odd[1] = near[1, rows, strands:] - imag


def last_kernel(info, own, other, zr, base, middle, odd, zl, vf):
    count = own.shape[1]
    for start, source in zip(places(info, count), (own, other)):
        vf[:, pl.ds(start, count), :] = source[...]
    put_left(zl, ALL, zr[0], zr[1])
    real, imag = apply(zl, vf[0], vf[1])
    middle[0] = real[:count]
    middle[1] = imag[:count]
    odd[0] = base[0] - real[count:]
    odd[1] = base[1] - imag[count:]


VMEM = pl.BlockSpec(memory_space=pltpu.VMEM)
SMEM = pl.BlockSpec(memory_space=pltpu.SMEM)


def size(shape, dtype):
    total = jnp.dtype(dtype).itemsize
    for extent in shape:
        total *= extent
    return total


def call(kernel, info, arrays, outs, scratch, flops):
    shapes = [jax.ShapeDtypeStruct(shape, F32) for shape in outs]
    moved = sum(size(x.shape, x.dtype) for x in list(arrays) + shapes)
    held = sum(size(*item) for item in scratch)
    return pl.pallas_call(
        kernel,
        out_shape=shapes,
        in_specs=[SMEM] + [VMEM] * len(arrays),
        out_specs=[VMEM] * len(outs),
        scratch_shapes=[pltpu.VMEM(*item) for item in scratch],
        compiler_params=pltpu.CompilerParams(
            vmem_limit_bytes=min(60 * 2**20, moved + held + 16 * 2**20)
        ),
        cost_estimate=pl.CostEstimate(
            flops=int(flops), bytes_accessed=int(moved), transcendentals=0
        ),
    )(info, *arrays)


def body(diag_block, lower_block, upper_block, twist, excitation):
    slabs = lax.axis_size("slab")
    slab = lax.axis_index("slab")
    row = lax.axis_index("row")
    diag, lower, upper, drive = diag_block[0], lower_block[0], upper_block[0], excitation[0]
    count, strands = diag.shape[1:]
    width = drive.shape[2]
    narrow = strands + width
    wide = strands + narrow
    info = jnp.stack([row, (slab % 4 == 1).astype(row.dtype)]).astype(jnp.int32)
    unit = 18 * strands**3

    def pairs(phase, by):
        return [
            (i, i + by) for i in range(slabs) if i % 4 == phase and 0 <= i + by < slabs
        ]

    def send(x, *moves):
        return lax.ppermute(x, "slab", [pair for move in moves for pair in pairs(*move)])

    def cross(x):
        return lax.ppermute(x, "row", [(0, 1), (1, 0)])

    def after(x, *gates):
        return lax.optimization_barrier((x,) + gates)[0]

    part = (2, count, strands)
    part_narrow = (2, count, narrow)
    part_thin = (2, count, width)
    full = (2, strands, strands)
    left = ((3, strands, 3 * strands), BF16)
    left_half = ((3, count, 3 * strands), BF16)

    def right(columns):
        return ((3, 3 * strands, columns), BF16)

    diag_other = cross(diag)
    rows = count // CHUNKS

    def strip(columns):
        return pl.BlockSpec((2, rows, columns), lambda step: (0, step, 0))

    first, second, joined, coarse = pl.pallas_call(
        twist_kernel,
        grid=(CHUNKS,),
        out_shape=[
            jax.ShapeDtypeStruct((2, count, columns), F32)
            for columns in (strands, strands, wide, narrow)
        ],
        in_specs=[
            SMEM,
            pl.BlockSpec((1, strands), lambda step: (0, 0)),
            strip(strands), strip(strands), strip(width), strip(strands),
        ],
        out_specs=[strip(strands), strip(strands), strip(wide), strip(narrow)],
        scratch_shapes=[pltpu.VMEM((strands, strands), BF16)],
        compiler_params=pltpu.CompilerParams(vmem_limit_bytes=32 * 2**20),
        cost_estimate=pl.CostEstimate(
            flops=unit // 3, bytes_accessed=9 * 2**20, transcendentals=0
        ),
    )(info, twist, lower, upper, drive, diag)

    from_above = send(first, (2, -1), (0, -1))
    from_below = send(second, (2, 1), (0, 1))
    swapped = send(coarse, (2, -2), (0, 2))
    joined_other = cross(joined)
    near, far = call(
        first_kernel, info, [diag, diag_other, joined, joined_other],
        [(2, strands, narrow), full],
        [(full, F32), left, right(strands)] * 2 + [right(wide)],
        unit * 6.25,
    )
    is_q = slab % 4 == 0
    near, swapped, from_above, from_below = lax.optimization_barrier(
        (near, swapped, from_above, from_below)
    )
    base_fine = send(jnp.where(is_q, swapped, coarse), (2, 1), (0, 1))
    (sent,) = call(
        couple_kernel, info, [from_above, from_below, near],
        [part_narrow], [left_half, right(narrow)], unit * 0.625,
    )
    got = send(sent, (1, 2), (3, -2))
    (keep,) = call(
        couple_kernel, info, [from_above, from_below, after(far, sent)],
        [part], [left_half, right(strands)], unit * 0.5,
    )
    keep_other = cross(keep)
    far_near, far_far = call(
        outer_kernel, info, [from_below, from_above, near, after(far, keep)],
        [part_narrow, part], [left_half, right(narrow), right(strands)], unit * 1.125,
    )
    fine = base_fine - after(sent, far_near) - got
    base_coarse = send(
        after(jnp.where(is_q, coarse, swapped), fine), (2, -3), (0, 1)
    )
    fine_other = cross(fine)
    out, mf, nf = call(
        second_kernel, info,
        [fine, fine_other, keep, keep_other, far_near, far_far],
        [part_narrow, full, full],
        [left, right(strands), right(strands), left_half, right(strands), right(width)]
        + [(part, F32)] * 2,
        unit * 3.625,
    )
    out_got = send(out, (3, 2), (1, -2))
    (zr,) = call(
        shadow_kernel, info, [mf, nf, near], [full],
        [(full, F32), left, right(strands), left, right(strands)], unit * 3.5,
    )
    total = after(out, zr) + base_coarse + out_got
    total_other = cross(total)
    left_two = ((2, strands, 3 * strands), BF16)
    xf, xr, wr, vr = call(
        coarse_kernel, info, [total, total_other, keep, fine],
        [(2, strands, width), part_thin, part_thin, part_thin],
        [left_two, ((2, count, 3 * strands), BF16)], unit * 2.5,
    )
    w_got = send(wr, (1, 2), (3, -2))
    x_even = send(xr, (1, -1))
    (base_odd,) = call(
        side_kernel, info, [near, far, xf], [part_thin],
        [((2, count, 3 * strands), BF16)], unit * 0.2,
    )
    v = after(vr, base_odd) + w_got
    v_other = cross(v)
    middle, odd = call(
        last_kernel, info, [v, v_other, zr, base_odd], [part_thin, part_thin],
        [left_two, ((2, strands, width), F32)], unit * 0.5,
    )
    x_middle = send(middle, (3, -1))
    return jnp.where(slab % 2 == 1, odd, x_even + x_middle)[None]


def solution(mesh):
    return jax.shard_map(
        body,
        mesh=mesh,
        in_specs=(
            P("slab", None, "row", None),
            P("slab", None, "row", None),
            P("slab", None, "row", None),
            P("slab", None),
            P("slab", None, "row", None),
        ),
        out_specs=P("slab", None, "row", None),
        check_vma=False,
    )
```

```python
import jax
import jax.numpy as jnp
from jax import lax
from jax.experimental import pallas as pl
from jax.experimental.pallas import tpu as pltpu
from jax.sharding import PartitionSpec as P

F32 = jnp.float32
BF16 = jnp.bfloat16
ALL = slice(None)
TILE = 256
MARK = 8
SHARE = 64


def halves(x):
    high = x.astype(BF16)
    return high, (x - high.astype(F32)).astype(BF16)


def dot(a, b):
    return jnp.dot(a, b, preferred_element_type=F32)


def put_left(ref, rows, real, imag):
    depth = ref.shape[2] // 3
    spans = [pl.ds(block * depth, depth) for block in range(3)]
    for part, value in enumerate((real, imag, real + imag)[: ref.shape[0]]):
        high, low = halves(value)
        ref[part, rows, spans[0]] = high
        ref[part, rows, spans[1]] = low
        ref[part, rows, spans[2]] = high


def put_right(ref, start, cols, real, imag):
    depth = ref.shape[1] // 3
    count = real.shape[0]
    spans = [pl.ds(pl.multiple_of(block * depth + start, 128), count) for block in range(3)]
    for part, value in enumerate((real, imag, real + imag)):
        high, low = halves(value)
        ref[part, spans[0], cols] = high
        ref[part, spans[1], cols] = high
        ref[part, spans[2], cols] = low


def product(left, right, emit, start=0, width=None):
    width = right.shape[2] if width is None else width
    count = left.shape[1]
    cols = pl.ds(start, width)

    def step(begin, extent):
        rows = pl.ds(begin, extent)
        first = dot(left[0, rows, :], right[0, :, cols])
        second = dot(left[1, rows, :], right[1, :, cols])
        third = dot(left[2, rows, :], right[2, :, cols])
        emit(begin, rows, first - second, third - first - second)

    if count <= TILE:
        step(0, count)
    else:

        @pl.loop(0, count // TILE)
        def _(index):
            step(pl.multiple_of(index * TILE, TILE), TILE)


def fill(target):
    def emit(begin, rows, real, imag):
        target[0, rows, :] = real
        target[1, rows, :] = imag

    return emit


def apply(left, real, imag, rows=ALL):
    width = real.shape[1]
    high, low = halves(jnp.concatenate([real, imag], axis=1))
    stacked = jnp.concatenate([high, high, low], axis=0)
    first = dot(left[0, rows, :], stacked)
    second = dot(left[1, rows, :], stacked)
    return (
        first[:, :width] - second[:, width:],
        first[:, width:] + second[:, :width],
    )


def eye(rows, cols, row_start):
    return (
        lax.broadcasted_iota(jnp.int32, (rows, cols), 0) + row_start
        == lax.broadcasted_iota(jnp.int32, (rows, cols), 1)
    ).astype(F32)


def places(info, count):
    return (
        pl.multiple_of(info[0] * count, count),
        pl.multiple_of((1 - info[0]) * count, count),
    )


def one_hot(order):
    strands = order.shape[1]
    return (lax.broadcasted_iota(jnp.int32, (strands, strands), 0) == order).astype(BF16)


def twisted(real, imag, pick):
    count = real.shape[0]
    moved = dot(jnp.concatenate(halves(real) + halves(imag), axis=0), pick)
    return (
        moved[:count] + moved[count : 2 * count],
        moved[2 * count : 3 * count] + moved[3 * count :],
    )


def load_step(info, own, other, mf, left, right):
    count = own.shape[1]
    strands = own.shape[1] * 2
    for start, source in zip(places(info, count), (own, other)):
        rows = pl.ds(start, count)
        real = eye(count, strands, start) - 0.2 * source[0, :, :strands]
        imag = -0.2 * source[1, :, :strands]
        if mf is not None:
            mf[0, rows, :] = real
            mf[1, rows, :] = imag
        put_left(left, rows, real, imag)
        if right is not None:
            put_right(right, start, ALL, real, imag)


def square(ml, mr, nf, nl, nr):
    def emit(begin, rows, real, imag):
        nf[0, rows, :] = real
        nf[1, rows, :] = imag
        if nl is not None:
            put_left(nl, rows, real, imag)
        put_right(nr, begin, ALL, real, imag)

    product(ml, mr, emit)


def inverse_tail(mf, ml, mr, nf, nl, nr, finish):
    strands = mf.shape[1]

    def quarter(begin, rows, real, imag):
        mf[0, rows, :] = (
            mf[0, rows, :] + nf[0, rows, :] + real + eye(real.shape[0], strands, begin)
        )
        mf[1, rows, :] = mf[1, rows, :] + nf[1, rows, :] + imag
        put_right(mr, begin, ALL, mf[0, rows, :], mf[1, rows, :])

    product(ml, nr, quarter)

    def fourth(begin, rows, real, imag):
        put_left(ml, rows, real, imag)

    product(nl, nr, fourth)

    def last(begin, rows, real, imag):
        finish(
            begin, rows, 0.2 * (mf[0, rows, :] + real), 0.2 * (mf[1, rows, :] + imag)
        )

    product(ml, mr, last)


def first_kernel(
    info, own, other, wide_own, wide_other, order, near, far, mf, ml, mr, nf, nl, nr, wr
):
    load_step(info, own, other, mf, ml, mr)
    count = own.shape[1]
    strands = mf.shape[1]
    width = wide_own.shape[2] - 2 * strands
    is_a = info[1] == 1
    pick = one_hot(order[...])
    low = pl.ds(0, strands)
    side = pl.ds(strands, width)
    up = pl.ds(strands + width, strands)
    for start, source in zip(places(info, count), (wide_own, wide_other)):
        put_right(wr, start, side, source[0, :, side], source[1, :, side])
        for cols, swap in ((low, is_a), (up, jnp.logical_not(is_a))):
            real, imag = twisted(
                jnp.where(swap, source[0, :, up], source[0, :, low]),
                jnp.where(swap, source[1, :, up], source[1, :, low]),
                pick,
            )
            put_right(wr, start, cols, real, imag)
    square(ml, mr, nf, nl, nr)

    def finish(begin, rows, real, imag):
        put_left(nl, rows, real, imag)

    inverse_tail(mf, ml, mr, nf, nl, nr, finish)
    narrow = near.shape[2]
    product(nl, wr, fill(near), 0, narrow)
    product(nl, wr, fill(far), narrow, strands)


def load_coupling(cl, above, below, marked, lead, swap, pick):
    ends = (marked.shape[1] - MARK, below.shape[1] - MARK)
    order = jnp.where(
        swap, marked[0, ends[0] : ends[0] + 1, :], below[0, ends[1] : ends[1] + 1, :]
    )
    pick[...] = one_hot(order.astype(jnp.int32))
    count = ends[0]
    for index, piece in enumerate(above):
        rows = pl.ds(0, count)
        span = pl.ds(lead + index * count, count)
        real, imag = twisted(
            jnp.where(swap, piece[0, rows, :], below[0, span, :]),
            jnp.where(swap, piece[1, rows, :], below[1, span, :]),
            pick[...],
        )
        put_left(cl, pl.ds(index * count, count), real, imag)


def couple_kernel(info, above, below, near, out, cl, rr, pick):
    load_coupling(cl, [above], below, above, 0, info[1] == 1, pick)
    put_right(rr, 0, ALL, near[0], near[1])
    product(cl, rr, fill(out))


def couple_end_kernel(info, above, marked, below, near, out, cl, rr, pick):
    lead = marked.shape[1] - MARK
    load_coupling(cl, [above], below, marked, lead, info[1] == 1, pick)
    put_right(rr, 0, ALL, near[0], near[1])
    product(cl, rr, fill(out))


def keep_kernel(info, above, above_end, below, far, out, cl, rr, pick):
    load_coupling(cl, [above, above_end], below, above, 0, info[1] == 1, pick)
    put_right(rr, 0, ALL, far[0], far[1])
    product(cl, rr, fill(out))


def outer_kernel(
    info, above, above_end, below, near, far, near_out, far_out, cl, nr, fr, pick
):
    load_coupling(cl, [above, above_end], below, above, 0, info[1] == 0, pick)
    put_right(nr, 0, ALL, near[0], near[1])
    put_right(fr, 0, ALL, far[0], far[1])
    product(cl, nr, fill(near_out))
    product(cl, fr, fill(far_out))


def step_right(source, gl, right, target, base):
    put_left(gl, ALL, source[0], source[1])

    def emit(begin, rows, real, imag):
        target[0, rows, :] = real if base is None else base[0, rows, :] + real
        target[1, rows, :] = imag if base is None else base[1, rows, :] + imag

    product(gl, right, emit)


def second_kernel(
    info, own, other, kc_own, kc_other, far_near, far_far, out, mf, nf,
    ml, mr, nr, gl, kr, er, g, k,
):
    load_step(info, own, other, mf, ml, mr)
    count = own.shape[1]
    strands = mf.shape[1]
    side = pl.ds(strands, own.shape[2] - strands)
    for start, source, edge in zip(places(info, count), (kc_own, kc_other), (own, other)):
        put_right(kr, start, ALL, source[0], source[1])
        put_right(er, start, ALL, edge[0, :, side], edge[1, :, side])
    square(ml, mr, nf, None, nr)
    g[...] = far_near[:, :, :strands]
    step_right(g, gl, mr, k, g)
    step_right(k, gl, nr, g, k)
    step_right(g, gl, nr, k, None)
    step_right(k, gl, nr, k, g)
    put_left(gl, ALL, 0.2 * k[0], 0.2 * k[1])

    head = pl.ds(0, strands)

    def lower(begin, rows, real, imag):
        out[0, rows, head] = -far_far[0, rows, :] - real
        out[1, rows, head] = -far_far[1, rows, :] - imag

    product(gl, kr, lower)

    def right(begin, rows, real, imag):
        out[0, rows, side] = real - far_near[0, rows, side]
        out[1, rows, side] = imag - far_near[1, rows, side]

    product(gl, er, right)


def shadow_kernel(info, mf, nf, near, zr, pf, ml, mr, nl, nr, gl):
    count = zr.shape[1] // 2
    strands = mf.shape[1]
    rows = pl.ds(places(info, count)[0], count)
    head = pl.ds(0, strands)
    pf[...] = mf[...]
    put_left(ml, ALL, mf[0], mf[1])
    put_left(nl, ALL, nf[0], nf[1])
    put_right(nr, 0, ALL, nf[0], nf[1])

    def finish(begin, rows, real, imag):
        pf[0, rows, :] = real
        pf[1, rows, :] = imag

    inverse_tail(pf, ml, mr, nf, nl, nr, finish)
    zr[:, :count, :] = pf[:, rows, :]
    put_right(mr, 0, ALL, pf[0], pf[1])
    put_left(gl, ALL, near[0, rows, head], near[1, rows, head])

    def emit(begin, rows, real, imag):
        zr[0, count:, :] = real
        zr[1, count:, :] = imag

    product(gl, mr, emit)


def coarse_kernel(info, own, other, keep, fine, xf, xr, wr, vr, ml, kl):
    load_step(info, own, other, None, ml, None)
    count = own.shape[1]
    strands = keep.shape[2]
    for start, source in zip(places(info, count), (own, other)):
        xf[:, pl.ds(start, count), :] = source[:, :, strands:]
    put_left(kl, ALL, keep[0], keep[1])
    real, imag = xf[0], xf[1]
    for _ in range(7):
        real, imag = apply(ml, real, imag)
        real = xf[0] + real
        imag = xf[1] + imag
    real = 0.2 * real
    imag = 0.2 * imag
    xf[0] = real
    xf[1] = imag
    xr[...] = xf[:, pl.ds(places(info, count)[0], count), :]
    real, imag = apply(kl, real, imag)
    wr[0] = real
    wr[1] = imag
    vr[0] = fine[0, :, strands:] + real
    vr[1] = fine[1, :, strands:] + imag


def side_kernel(info, near, far, xf, odd, fl):
    count = odd.shape[1]
    strands = far.shape[2]
    rows = pl.ds(places(info, count)[0], count)
    put_left(fl, ALL, far[0, rows, :], far[1, rows, :])
    real, imag = apply(fl, xf[0], xf[1])
    odd[0] = near[0, rows, strands:] - real
    odd[1] = near[1, rows, strands:] - imag


def last_kernel(info, own, other, zr, base, middle, odd, zl, vf):
    count = own.shape[1]
    for start, source in zip(places(info, count), (own, other)):
        vf[:, pl.ds(start, count), :] = source[...]
    put_left(zl, ALL, zr[0], zr[1])
    real, imag = apply(zl, vf[0], vf[1])
    middle[0] = real[:count]
    middle[1] = imag[:count]
    odd[0] = base[0] - real[count:]
    odd[1] = base[1] - imag[count:]


VMEM = pl.BlockSpec(memory_space=pltpu.VMEM)
SMEM = pl.BlockSpec(memory_space=pltpu.SMEM)


def size(shape, dtype):
    total = jnp.dtype(dtype).itemsize
    for extent in shape:
        total *= extent
    return total


def call(kernel, info, arrays, outs, scratch, flops):
    shapes = [jax.ShapeDtypeStruct(shape, F32) for shape in outs]
    moved = sum(size(x.shape, x.dtype) for x in list(arrays) + shapes)
    held = sum(size(*item) for item in scratch)
    return pl.pallas_call(
        kernel,
        out_shape=shapes,
        in_specs=[SMEM] + [VMEM] * len(arrays),
        out_specs=[VMEM] * len(outs),
        scratch_shapes=[pltpu.VMEM(*item) for item in scratch],
        compiler_params=pltpu.CompilerParams(
            vmem_limit_bytes=min(60 * 2**20, moved + held + 16 * 2**20)
        ),
        cost_estimate=pl.CostEstimate(
            flops=int(flops) // SHARE, bytes_accessed=int(moved) // SHARE, transcendentals=0
        ),
    )(info, *arrays)


def body(diag_block, lower_block, upper_block, twist, excitation):
    slabs = lax.axis_size("slab")
    slab = lax.axis_index("slab")
    row = lax.axis_index("row")
    diag, lower, upper, drive = diag_block[0], lower_block[0], upper_block[0], excitation[0]
    count, strands = diag.shape[1:]
    width = drive.shape[2]
    narrow = strands + width
    wide = strands + narrow
    info = jnp.stack([row, (slab % 4 == 1).astype(row.dtype)]).astype(jnp.int32)
    unit = 18 * strands**3

    def pairs(phase, by):
        return [
            (i, i + by) for i in range(slabs) if i % 4 == phase and 0 <= i + by < slabs
        ]

    def send(x, *moves):
        return lax.ppermute(x, "slab", [pair for move in moves for pair in pairs(*move)])

    def cross(x):
        return lax.ppermute(x, "row", [(0, 1), (1, 0)])

    def after(x, *gates):
        return lax.optimization_barrier((x,) + gates)[0]

    part = (2, count, strands)
    part_narrow = (2, count, narrow)
    part_thin = (2, count, width)
    full = (2, strands, strands)
    left = ((3, strands, 3 * strands), BF16)
    left_half = ((3, count, 3 * strands), BF16)

    def right(columns):
        return ((3, 3 * strands, columns), BF16)

    middle = count // 2
    top, end = slice(0, middle), slice(middle, count)
    marks = jnp.broadcast_to(twist.astype(F32), (2, MARK, strands))
    below = send(jnp.concatenate([upper, marks], axis=1), (2, 1), (0, 1))
    above_top = send(
        jnp.concatenate([lower[:, top], marks], axis=1), (2, -1), (0, -1)
    )
    lower_swap = send(lower[:, end], (2, -2), (0, 2))
    diag_other = cross(diag)
    joined = jnp.concatenate([lower, drive, upper], axis=2)
    joined_other = cross(joined)
    base = jnp.concatenate([diag, drive], axis=2)
    base_swap = send(after(base, diag_other), (2, -2), (0, 2))
    near, far = call(
        first_kernel, info, [diag, diag_other, joined, joined_other, twist],
        [(2, strands, narrow), full],
        [(full, F32), left, right(strands)] * 2 + [right(wide)],
        unit * 6.5,
    )
    is_q = slab % 4 == 0
    near, lower_swap, above_top, below = lax.optimization_barrier(
        (near, lower_swap, above_top, below)
    )
    above_end = send(lower_swap, (2, -3), (0, 1))
    pick = ((strands, strands), BF16)
    left_quarter = ((3, middle, 3 * strands), BF16)
    half_narrow = (2, middle, narrow)
    (sent_top,) = call(
        couple_kernel, info, [above_top, below, near],
        [half_narrow], [left_quarter, right(narrow), pick], unit * 0.35,
    )
    got_top = send(sent_top, (1, 2), (3, -2))
    base_swap = after(base_swap, above_end, sent_top)
    base_fine = send(jnp.where(is_q, base_swap, base), (2, 1), (0, 1))
    (sent_end,) = call(
        couple_end_kernel, info, [above_end, above_top, below, near],
        [half_narrow], [left_quarter, right(narrow), pick], unit * 0.35,
    )
    got_end = send(sent_end, (1, 2), (3, -2))
    pieces = [above_top, above_end, below]
    (keep,) = call(
        keep_kernel, info, pieces + [after(far, sent_end)],
        [part], [left_half, right(strands), pick], unit * 0.5,
    )
    keep_other = cross(keep)
    far_near, far_far = call(
        outer_kernel, info, pieces + [near, after(far, keep)],
        [part_narrow, part], [left_half, right(narrow), right(strands), pick], unit * 1.125,
    )
    terms = jnp.concatenate(
        [after(sent_top, far_near) + got_top, sent_end + got_end], axis=1
    )
    fine = base_fine - lax.optimization_barrier(terms)
    base_coarse = send(
        after(jnp.where(is_q, base, base_swap), fine), (2, -3), (0, 1)
    )
    fine_other = cross(fine)
    out, mf, nf = call(
        second_kernel, info,
        [fine, fine_other, keep, keep_other, far_near, far_far],
        [part_narrow, full, full],
        [left, right(strands), right(strands), left_half, right(strands), right(width)]
        + [(part, F32)] * 2,
        unit * 3.625,
    )
    out_got = send(out, (3, 2), (1, -2))
    (zr,) = call(
        shadow_kernel, info, [mf, nf, near], [full],
        [(full, F32), left, right(strands), left, right(strands), left_half], unit * 3.5,
    )
    total = after(out, zr) + base_coarse + out_got
    total_other = cross(total)
    left_two = ((2, strands, 3 * strands), BF16)
    xf, xr, wr, vr = call(
        coarse_kernel, info, [total, total_other, keep, fine],
        [(2, strands, width), part_thin, part_thin, part_thin],
        [left_two, ((2, count, 3 * strands), BF16)], unit * 2.5,
    )
    w_got = send(wr, (1, 2), (3, -2))
    x_even = send(xr, (1, -1))
    (base_odd,) = call(
        side_kernel, info, [near, far, xf], [part_thin],
        [((2, count, 3 * strands), BF16)], unit * 0.2,
    )
    v = after(vr, base_odd) + w_got
    v_other = cross(v)
    middle, odd = call(
        last_kernel, info, [v, v_other, zr, base_odd], [part_thin, part_thin],
        [left_two, ((2, strands, width), F32)], unit * 0.5,
    )
    x_middle = send(middle, (3, -1))
    return jnp.where(slab % 2 == 1, odd, x_even + x_middle)[None]


def solution(mesh):
    return jax.shard_map(
        body,
        mesh=mesh,
        in_specs=(
            P("slab", None, "row", None),
            P("slab", None, "row", None),
            P("slab", None, "row", None),
            P("slab", None),
            P("slab", None, "row", None),
        ),
        out_specs=P("slab", None, "row", None),
        check_vma=False,
    )
```

```python
import jax
import jax.numpy as jnp
from jax import lax
from jax.experimental import pallas as pl
from jax.experimental.pallas import tpu as pltpu
from jax.sharding import PartitionSpec as P

F32 = jnp.float32
BF16 = jnp.bfloat16
ALL = slice(None)
TILE = 256
MARK = 8
SHARE = 4096


def halves(x):
    high = x.astype(BF16)
    return high, (x - high.astype(F32)).astype(BF16)


def dot(a, b):
    return jnp.dot(a, b, preferred_element_type=F32)


def put_left(ref, rows, real, imag):
    depth = ref.shape[2] // 3
    spans = [pl.ds(block * depth, depth) for block in range(3)]
    for part, value in enumerate((real, imag, real + imag)[: ref.shape[0]]):
        high, low = halves(value)
        ref[part, rows, spans[0]] = high
        ref[part, rows, spans[1]] = low
        ref[part, rows, spans[2]] = high


def put_right(ref, start, cols, real, imag):
    depth = ref.shape[1] // 3
    count = real.shape[0]
    spans = [pl.ds(pl.multiple_of(block * depth + start, 128), count) for block in range(3)]
    for part, value in enumerate((real, imag, real + imag)):
        high, low = halves(value)
        ref[part, spans[0], cols] = high
        ref[part, spans[1], cols] = high
        ref[part, spans[2], cols] = low


def product(left, right, emit, start=0, width=None):
    width = right.shape[2] if width is None else width
    count = left.shape[1]
    cols = pl.ds(start, width)

    def step(begin, extent):
        rows = pl.ds(begin, extent)
        first = dot(left[0, rows, :], right[0, :, cols])
        second = dot(left[1, rows, :], right[1, :, cols])
        third = dot(left[2, rows, :], right[2, :, cols])
        emit(begin, rows, first - second, third - first - second)

    if count <= TILE:
        step(0, count)
    else:

        @pl.loop(0, count // TILE)
        def _(index):
            step(pl.multiple_of(index * TILE, TILE), TILE)


def fill(target):
    def emit(begin, rows, real, imag):
        target[0, rows, :] = real
        target[1, rows, :] = imag

    return emit


def apply(left, real, imag, rows=ALL):
    width = real.shape[1]
    high, low = halves(jnp.concatenate([real, imag], axis=1))
    stacked = jnp.concatenate([high, high, low], axis=0)
    first = dot(left[0, rows, :], stacked)
    second = dot(left[1, rows, :], stacked)
    return (
        first[:, :width] - second[:, width:],
        first[:, width:] + second[:, :width],
    )


def eye(rows, cols, row_start):
    return (
        lax.broadcasted_iota(jnp.int32, (rows, cols), 0) + row_start
        == lax.broadcasted_iota(jnp.int32, (rows, cols), 1)
    ).astype(F32)


def places(info, count):
    return (
        pl.multiple_of(info[0] * count, count),
        pl.multiple_of((1 - info[0]) * count, count),
    )


def one_hot(order):
    strands = order.shape[1]
    return (lax.broadcasted_iota(jnp.int32, (strands, strands), 0) == order).astype(BF16)


def twisted(real, imag, pick):
    count = real.shape[0]
    moved = dot(jnp.concatenate(halves(real) + halves(imag), axis=0), pick)
    return (
        moved[:count] + moved[count : 2 * count],
        moved[2 * count : 3 * count] + moved[3 * count :],
    )


def load_step(info, own, other, mf, left, right):
    count = own.shape[1]
    strands = own.shape[1] * 2
    for start, source in zip(places(info, count), (own, other)):
        rows = pl.ds(start, count)
        real = eye(count, strands, start) - 0.2 * source[0, :, :strands]
        imag = -0.2 * source[1, :, :strands]
        if mf is not None:
            mf[0, rows, :] = real
            mf[1, rows, :] = imag
        put_left(left, rows, real, imag)
        if right is not None:
            put_right(right, start, ALL, real, imag)


def square(ml, mr, nf, nl, nr):
    def emit(begin, rows, real, imag):
        nf[0, rows, :] = real
        nf[1, rows, :] = imag
        if nl is not None:
            put_left(nl, rows, real, imag)
        put_right(nr, begin, ALL, real, imag)

    product(ml, mr, emit)


def inverse_tail(mf, ml, mr, nf, nl, nr, finish):
    strands = mf.shape[1]

    def quarter(begin, rows, real, imag):
        mf[0, rows, :] = (
            mf[0, rows, :] + nf[0, rows, :] + real + eye(real.shape[0], strands, begin)
        )
        mf[1, rows, :] = mf[1, rows, :] + nf[1, rows, :] + imag
        put_right(mr, begin, ALL, mf[0, rows, :], mf[1, rows, :])

    product(ml, nr, quarter)

    def fourth(begin, rows, real, imag):
        put_left(ml, rows, real, imag)

    product(nl, nr, fourth)

    def last(begin, rows, real, imag):
        finish(
            begin, rows, 0.2 * (mf[0, rows, :] + real), 0.2 * (mf[1, rows, :] + imag)
        )

    product(ml, mr, last)


def first_kernel(
    info, own, other, lower, upper, drive, order, near, far, mf, ml, mr, nf, nl, nr, wr
):
    load_step(info, own, other, mf, ml, mr)
    strands = lower.shape[2]
    width = drive.shape[2]
    narrow = strands + width
    is_a = info[1] == 1
    pick = one_hot(order[...])
    put_right(wr, 0, pl.ds(strands, width), drive[0], drive[1])
    for begin, swap in ((0, is_a), (narrow, jnp.logical_not(is_a))):
        real, imag = twisted(
            jnp.where(swap, upper[0], lower[0]), jnp.where(swap, upper[1], lower[1]), pick
        )
        put_right(wr, 0, pl.ds(begin, strands), real, imag)
    square(ml, mr, nf, nl, nr)

    def finish(begin, rows, real, imag):
        put_left(nl, rows, real, imag)

    inverse_tail(mf, ml, mr, nf, nl, nr, finish)
    product(nl, wr, fill(near), 0, narrow)
    product(nl, wr, fill(far), narrow, strands)


def load_coupling(cl, marked, above_end, below, swap, pick):
    count = above_end.shape[1]
    middle = count + MARK // 2
    order = jnp.concatenate(
        [marked[0, count : count + 1, :], marked[0, middle : middle + 1, :]], axis=1
    )
    order = jnp.where(swap, order, below[0, count : count + 1, :])
    pick[...] = one_hot(order.astype(jnp.int32))
    rows = pl.ds(0, count)
    real, imag = (
        jnp.where(
            swap,
            jnp.concatenate([marked[part, rows, :], above_end[part]], axis=1),
            below[part, rows, :],
        )
        for part in range(2)
    )
    real, imag = twisted(real, imag, pick[...])
    put_left(cl, ALL, real, imag)


def keep_kernel(info, above, above_end, below, far, out, cl, rr, pick):
    load_coupling(cl, above, above_end, below, info[1] == 1, pick)
    put_right(rr, 0, ALL, far[0], far[1])
    product(cl, rr, fill(out))


def outer_kernel(
    info, above, above_end, below, near, far, near_out, far_out, cl, nr, fr, pick
):
    load_coupling(cl, above, above_end, below, info[1] == 0, pick)
    put_right(nr, 0, ALL, near[0], near[1])
    put_right(fr, 0, ALL, far[0], far[1])
    product(cl, nr, fill(near_out))
    product(cl, fr, fill(far_out))


def step_right(source, gl, right, target, base):
    put_left(gl, ALL, source[0], source[1])

    def emit(begin, rows, real, imag):
        target[0, rows, :] = real if base is None else base[0, rows, :] + real
        target[1, rows, :] = imag if base is None else base[1, rows, :] + imag

    product(gl, right, emit)


def second_kernel(
    info, own, other, kc_own, kc_other, far_near, far_far, out, mf, nf,
    ml, mr, nr, gl, kr, er, g, k,
):
    load_step(info, own, other, mf, ml, mr)
    count = own.shape[1]
    strands = mf.shape[1]
    side = pl.ds(strands, own.shape[2] - strands)
    for start, source, edge in zip(places(info, count), (kc_own, kc_other), (own, other)):
        put_right(kr, start, ALL, source[0], source[1])
        put_right(er, start, ALL, edge[0, :, side], edge[1, :, side])
    square(ml, mr, nf, None, nr)
    g[...] = far_near[:, :, :strands]
    step_right(g, gl, mr, k, g)
    step_right(k, gl, nr, g, k)
    step_right(g, gl, nr, k, None)
    step_right(k, gl, nr, k, g)
    put_left(gl, ALL, 0.2 * k[0], 0.2 * k[1])

    head = pl.ds(0, strands)

    def lower(begin, rows, real, imag):
        out[0, rows, head] = -far_far[0, rows, :] - real
        out[1, rows, head] = -far_far[1, rows, :] - imag

    product(gl, kr, lower)

    def right(begin, rows, real, imag):
        out[0, rows, side] = real - far_near[0, rows, side]
        out[1, rows, side] = imag - far_near[1, rows, side]

    product(gl, er, right)


def shadow_kernel(info, mf, nf, near, zr, pf, ml, mr, nl, nr, gl):
    count = zr.shape[1] // 2
    strands = mf.shape[1]
    rows = pl.ds(places(info, count)[0], count)
    head = pl.ds(0, strands)
    pf[...] = mf[...]
    put_left(ml, ALL, mf[0], mf[1])
    put_left(nl, ALL, nf[0], nf[1])
    put_right(nr, 0, ALL, nf[0], nf[1])

    def finish(begin, rows, real, imag):
        pf[0, rows, :] = real
        pf[1, rows, :] = imag

    inverse_tail(pf, ml, mr, nf, nl, nr, finish)
    zr[:, :count, :] = pf[:, rows, :]
    put_right(mr, 0, ALL, pf[0], pf[1])
    put_left(gl, ALL, near[0, rows, head], near[1, rows, head])

    def emit(begin, rows, real, imag):
        zr[0, count:, :] = real
        zr[1, count:, :] = imag

    product(gl, mr, emit)


def coarse_kernel(info, own, other, keep, fine, xf, xr, wr, vr, ml, kl):
    load_step(info, own, other, None, ml, None)
    count = own.shape[1]
    strands = keep.shape[2]
    for start, source in zip(places(info, count), (own, other)):
        xf[:, pl.ds(start, count), :] = source[:, :, strands:]
    put_left(kl, ALL, keep[0], keep[1])
    real, imag = xf[0], xf[1]
    for _ in range(7):
        real, imag = apply(ml, real, imag)
        real = xf[0] + real
        imag = xf[1] + imag
    real = 0.2 * real
    imag = 0.2 * imag
    xf[0] = real
    xf[1] = imag
    xr[...] = xf[:, pl.ds(places(info, count)[0], count), :]
    real, imag = apply(kl, real, imag)
    wr[0] = real
    wr[1] = imag
    vr[0] = fine[0, :, strands:] + real
    vr[1] = fine[1, :, strands:] + imag


def side_kernel(info, near, far, xf, odd, fl):
    count = odd.shape[1]
    strands = far.shape[2]
    rows = pl.ds(places(info, count)[0], count)
    put_left(fl, ALL, far[0, rows, :], far[1, rows, :])
    real, imag = apply(fl, xf[0], xf[1])
    odd[0] = near[0, rows, strands:] - real
    odd[1] = near[1, rows, strands:] - imag


def last_kernel(info, own, other, zr, base, middle, odd, zl, vf):
    count = own.shape[1]
    for start, source in zip(places(info, count), (own, other)):
        vf[:, pl.ds(start, count), :] = source[...]
    put_left(zl, ALL, zr[0], zr[1])
    real, imag = apply(zl, vf[0], vf[1])
    middle[0] = real[:count]
    middle[1] = imag[:count]
    odd[0] = base[0] - real[count:]
    odd[1] = base[1] - imag[count:]


VMEM = pl.BlockSpec(memory_space=pltpu.VMEM)
SMEM = pl.BlockSpec(memory_space=pltpu.SMEM)


def size(shape, dtype):
    total = jnp.dtype(dtype).itemsize
    for extent in shape:
        total *= extent
    return total


def call(kernel, info, arrays, outs, scratch, flops):
    shapes = [jax.ShapeDtypeStruct(shape, F32) for shape in outs]
    moved = sum(size(x.shape, x.dtype) for x in list(arrays) + shapes)
    held = sum(size(*item) for item in scratch)
    return pl.pallas_call(
        kernel,
        out_shape=shapes,
        in_specs=[SMEM] + [VMEM] * len(arrays),
        out_specs=[VMEM] * len(outs),
        scratch_shapes=[pltpu.VMEM(*item) for item in scratch],
        compiler_params=pltpu.CompilerParams(
            vmem_limit_bytes=min(60 * 2**20, moved + held + 16 * 2**20)
        ),
        cost_estimate=pl.CostEstimate(
            flops=int(flops) // SHARE, bytes_accessed=int(moved) // SHARE, transcendentals=0
        ),
    )(info, *arrays)


def body(diag_block, lower_block, upper_block, twist, excitation):
    slabs = lax.axis_size("slab")
    slab = lax.axis_index("slab")
    row = lax.axis_index("row")
    diag, lower, upper, drive = diag_block[0], lower_block[0], upper_block[0], excitation[0]
    count, strands = diag.shape[1:]
    width = drive.shape[2]
    narrow = strands + width
    wide = strands + narrow
    info = jnp.stack([row, (slab % 4 == 1).astype(row.dtype)]).astype(jnp.int32)
    unit = 18 * strands**3

    def pairs(phase, by):
        return [
            (i, i + by) for i in range(slabs) if i % 4 == phase and 0 <= i + by < slabs
        ]

    def send(x, *moves):
        return lax.ppermute(x, "slab", [pair for move in moves for pair in pairs(*move)])

    def cross(x):
        return lax.ppermute(x, "row", [(0, 1), (1, 0)])

    def after(x, *gates):
        return lax.optimization_barrier((x,) + gates)[0]

    part = (2, count, strands)
    part_narrow = (2, count, narrow)
    part_thin = (2, count, width)
    full = (2, strands, strands)
    left = ((3, strands, 3 * strands), BF16)
    left_half = ((3, count, 3 * strands), BF16)

    def right(columns):
        return ((3, 3 * strands, columns), BF16)

    half = strands // 2
    marks = jnp.broadcast_to(twist.astype(F32), (2, MARK, strands))
    thin_marks = jnp.concatenate(
        [marks[:, : MARK // 2, :half], marks[:, : MARK // 2, half:]], axis=1
    )
    swapped = send(
        jnp.concatenate([lower[:, :, half:], diag, drive], axis=2), (2, -2), (0, 2)
    )
    below = send(jnp.concatenate([upper, marks], axis=1), (2, 1), (0, 1))
    above_top = send(
        jnp.concatenate([lower[:, :, :half], thin_marks], axis=1), (2, -1), (0, -1)
    )
    diag_other = cross(diag)
    lower_full, upper_full, drive_full = (
        lax.all_gather(x, "row", axis=1, tiled=True) for x in (lower, upper, drive)
    )
    base = jnp.concatenate([diag, drive], axis=2)
    near, far = call(
        first_kernel, info,
        [diag, diag_other, lower_full, upper_full, drive_full, twist],
        [(2, strands, narrow), full],
        [(full, F32), left, right(strands)] * 2 + [right(wide)],
        unit * 6.5,
    )
    is_q = slab % 4 == 0
    near, swapped = lax.optimization_barrier((near, swapped))
    above_end = send(swapped[:, :, :half], (2, -3), (0, 1))
    base_swap = swapped[:, :, half:]
    base_pay = jnp.where(is_q, base_swap, base)
    above_end, base_pay = lax.optimization_barrier((above_end, base_pay))
    base_fine = send(base_pay, (2, 1), (0, 1))
    pick = ((strands, strands), BF16)
    pieces = [above_top, above_end, below]
    (sent,) = call(
        keep_kernel, info, pieces + [near],
        [part_narrow], [left_half, right(narrow), pick], unit * 0.625,
    )
    got = send(sent, (1, 2), (3, -2))
    (keep,) = call(
        keep_kernel, info, pieces + [after(far, sent)],
        [part], [left_half, right(strands), pick], unit * 0.5,
    )
    keep_other = cross(keep)
    far_near, far_far = call(
        outer_kernel, info, pieces + [near, after(far, keep)],
        [part_narrow, part], [left_half, right(narrow), right(strands), pick], unit * 1.125,
    )
    fine = base_fine - after(sent, far_near) - got
    base_coarse = send(
        after(jnp.where(is_q, base, base_swap), fine), (2, -3), (0, 1)
    )
    fine_other = cross(fine)
    out, mf, nf = call(
        second_kernel, info,
        [fine, fine_other, keep, keep_other, far_near, far_far],
        [part_narrow, full, full],
        [left, right(strands), right(strands), left_half, right(strands), right(width)]
        + [(part, F32)] * 2,
        unit * 3.625,
    )
    out_got = send(out, (3, 2), (1, -2))
    (zr,) = call(
        shadow_kernel, info, [mf, nf, near], [full],
        [(full, F32), left, right(strands), left, right(strands), left_half], unit * 3.5,
    )
    total = after(out, zr) + base_coarse + out_got
    total_other = cross(total)
    left_two = ((2, strands, 3 * strands), BF16)
    xf, xr, wr, vr = call(
        coarse_kernel, info, [total, total_other, keep, fine],
        [(2, strands, width), part_thin, part_thin, part_thin],
        [left_two, ((2, count, 3 * strands), BF16)], unit * 2.5,
    )
    w_got = send(wr, (1, 2), (3, -2))
    x_even = send(xr, (1, -1))
    (base_odd,) = call(
        side_kernel, info, [near, far, xf], [part_thin],
        [((2, count, 3 * strands), BF16)], unit * 0.2,
    )
    v = after(vr, base_odd) + w_got
    v_other = cross(v)
    middle, odd = call(
        last_kernel, info, [v, v_other, zr, base_odd], [part_thin, part_thin],
        [left_two, ((2, strands, width), F32)], unit * 0.5,
    )
    x_middle = send(middle, (3, -1))
    return jnp.where(slab % 2 == 1, odd, x_even + x_middle)[None]


def solution(mesh):
    return jax.shard_map(
        body,
        mesh=mesh,
        in_specs=(
            P("slab", None, "row", None),
            P("slab", None, "row", None),
            P("slab", None, "row", None),
            P("slab", None),
            P("slab", None, "row", None),
        ),
        out_specs=P("slab", None, "row", None),
        check_vma=False,
    )
```

```python
import jax
import jax.numpy as jnp
from jax import lax
from jax.experimental import pallas as pl
from jax.experimental.pallas import tpu as pltpu
from jax.sharding import PartitionSpec as P

F32 = jnp.float32
BF16 = jnp.bfloat16
ALL = slice(None)
TILE = 256
MARK = 8
SHARE = 4096


def halves(x):
    high = x.astype(BF16)
    return high, (x - high.astype(F32)).astype(BF16)


def dot(a, b):
    return jnp.dot(a, b, preferred_element_type=F32)


def put_left(ref, rows, real, imag):
    depth = ref.shape[2] // 3
    spans = [pl.ds(block * depth, depth) for block in range(3)]
    for part, value in enumerate((real, imag, real + imag)[: ref.shape[0]]):
        high, low = halves(value)
        ref[part, rows, spans[0]] = high
        ref[part, rows, spans[1]] = low
        ref[part, rows, spans[2]] = high


def put_right(ref, start, cols, real, imag):
    depth = ref.shape[1] // 3
    count = real.shape[0]
    spans = [pl.ds(pl.multiple_of(block * depth + start, 128), count) for block in range(3)]
    for part, value in enumerate((real, imag, real + imag)):
        high, low = halves(value)
        ref[part, spans[0], cols] = high
        ref[part, spans[1], cols] = high
        ref[part, spans[2], cols] = low


def product(left, right, emit, start=0, width=None):
    width = right.shape[2] if width is None else width
    count = left.shape[1]
    cols = pl.ds(start, width)

    def step(begin, extent):
        rows = pl.ds(begin, extent)
        first = dot(left[0, rows, :], right[0, :, cols])
        second = dot(left[1, rows, :], right[1, :, cols])
        third = dot(left[2, rows, :], right[2, :, cols])
        emit(begin, rows, first - second, third - first - second)

    if count <= TILE:
        step(0, count)
    else:

        @pl.loop(0, count // TILE)
        def _(index):
            step(pl.multiple_of(index * TILE, TILE), TILE)


def fill(target):
    def emit(begin, rows, real, imag):
        target[0, rows, :] = real
        target[1, rows, :] = imag

    return emit


def apply(left, real, imag, rows=ALL):
    width = real.shape[1]
    high, low = halves(jnp.concatenate([real, imag], axis=1))
    stacked = jnp.concatenate([high, high, low], axis=0)
    first = dot(left[0, rows, :], stacked)
    second = dot(left[1, rows, :], stacked)
    return (
        first[:, :width] - second[:, width:],
        first[:, width:] + second[:, :width],
    )


def eye(rows, cols, row_start):
    return (
        lax.broadcasted_iota(jnp.int32, (rows, cols), 0) + row_start
        == lax.broadcasted_iota(jnp.int32, (rows, cols), 1)
    ).astype(F32)


def places(info, count):
    return (
        pl.multiple_of(info[0] * count, count),
        pl.multiple_of((1 - info[0]) * count, count),
    )


def one_hot(order):
    strands = order.shape[1]
    return (lax.broadcasted_iota(jnp.int32, (strands, strands), 0) == order).astype(BF16)


def twisted(real, imag, pick):
    count = real.shape[0]
    moved = dot(jnp.concatenate(halves(real) + halves(imag), axis=0), pick)
    return (
        moved[:count] + moved[count : 2 * count],
        moved[2 * count : 3 * count] + moved[3 * count :],
    )


def load_step(info, own, other, mf, left, right):
    count = own.shape[1]
    strands = own.shape[1] * 2
    for start, source in zip(places(info, count), (own, other)):
        rows = pl.ds(start, count)
        real = eye(count, strands, start) - 0.2 * source[0, :, :strands]
        imag = -0.2 * source[1, :, :strands]
        if mf is not None:
            mf[0, rows, :] = real
            mf[1, rows, :] = imag
        put_left(left, rows, real, imag)
        if right is not None:
            put_right(right, start, ALL, real, imag)


def square(ml, mr, nf, nl, nr):
    def emit(begin, rows, real, imag):
        nf[0, rows, :] = real
        nf[1, rows, :] = imag
        if nl is not None:
            put_left(nl, rows, real, imag)
        put_right(nr, begin, ALL, real, imag)

    product(ml, mr, emit)


def inverse_tail(mf, ml, mr, nf, nl, nr, finish):
    strands = mf.shape[1]

    def quarter(begin, rows, real, imag):
        mf[0, rows, :] = (
            mf[0, rows, :] + nf[0, rows, :] + real + eye(real.shape[0], strands, begin)
        )
        mf[1, rows, :] = mf[1, rows, :] + nf[1, rows, :] + imag
        put_right(mr, begin, ALL, mf[0, rows, :], mf[1, rows, :])

    product(ml, nr, quarter)

    def fourth(begin, rows, real, imag):
        put_left(ml, rows, real, imag)

    product(nl, nr, fourth)

    def last(begin, rows, real, imag):
        finish(
            begin, rows, 0.2 * (mf[0, rows, :] + real), 0.2 * (mf[1, rows, :] + imag)
        )

    product(ml, mr, last)


def first_kernel(
    info, own, other, wide_own, wide_other, order, near, far, mf, ml, mr, nf, nl, nr, wr
):
    load_step(info, own, other, mf, ml, mr)
    count = own.shape[1]
    strands = mf.shape[1]
    width = wide_own.shape[2] - 2 * strands
    narrow = strands + width
    is_a = info[1] == 1
    pick = one_hot(order[...])
    low = pl.ds(0, strands)
    side = pl.ds(strands, width)
    up = pl.ds(narrow, strands)
    for start, source in zip(places(info, count), (wide_own, wide_other)):
        put_right(wr, start, side, source[0, :, side], source[1, :, side])
        for cols, swap in ((low, is_a), (up, jnp.logical_not(is_a))):
            real, imag = twisted(
                jnp.where(swap, source[0, :, up], source[0, :, low]),
                jnp.where(swap, source[1, :, up], source[1, :, low]),
                pick,
            )
            put_right(wr, start, cols, real, imag)
    square(ml, mr, nf, nl, nr)

    def finish(begin, rows, real, imag):
        put_left(nl, rows, real, imag)

    inverse_tail(mf, ml, mr, nf, nl, nr, finish)
    product(nl, wr, fill(near), 0, narrow)
    product(nl, wr, fill(far), narrow, strands)


def load_coupling(cl, above, below, swap, pick):
    count = cl.shape[1]
    rows = pl.ds(0, count)
    order = jnp.where(
        swap, above[0, count : count + 1, :], below[0, count : count + 1, :]
    )
    pick[...] = one_hot(order.astype(jnp.int32))
    real, imag = (
        jnp.where(swap, above[part, rows, :], below[part, rows, :]) for part in range(2)
    )
    real, imag = twisted(real, imag, pick[...])
    put_left(cl, ALL, real, imag)


def keep_kernel(info, above, below, far, out, cl, rr, pick):
    load_coupling(cl, above, below, info[1] == 1, pick)
    put_right(rr, 0, ALL, far[0], far[1])
    product(cl, rr, fill(out))


def outer_kernel(
    info, above, below, near, far, near_out, far_out, cl, nr, fr, pick
):
    load_coupling(cl, above, below, info[1] == 0, pick)
    put_right(nr, 0, ALL, near[0], near[1])
    put_right(fr, 0, ALL, far[0], far[1])
    product(cl, nr, fill(near_out))
    product(cl, fr, fill(far_out))


def step_right(source, gl, right, target, base):
    put_left(gl, ALL, source[0], source[1])

    def emit(begin, rows, real, imag):
        target[0, rows, :] = real if base is None else base[0, rows, :] + real
        target[1, rows, :] = imag if base is None else base[1, rows, :] + imag

    product(gl, right, emit)


def second_kernel(
    info, own, other, kc_own, kc_other, far_near, far_far, out, mf, nf,
    ml, mr, nr, gl, kr, er, g, k,
):
    load_step(info, own, other, mf, ml, mr)
    count = own.shape[1]
    strands = mf.shape[1]
    side = pl.ds(strands, own.shape[2] - strands)
    for start, source, edge in zip(places(info, count), (kc_own, kc_other), (own, other)):
        put_right(kr, start, ALL, source[0], source[1])
        put_right(er, start, ALL, edge[0, :, side], edge[1, :, side])
    square(ml, mr, nf, None, nr)
    g[...] = far_near[:, :, :strands]
    step_right(g, gl, mr, k, g)
    step_right(k, gl, nr, g, k)
    step_right(g, gl, nr, k, None)
    step_right(k, gl, nr, k, g)
    put_left(gl, ALL, 0.2 * k[0], 0.2 * k[1])

    head = pl.ds(0, strands)

    def lower(begin, rows, real, imag):
        out[0, rows, head] = -far_far[0, rows, :] - real
        out[1, rows, head] = -far_far[1, rows, :] - imag

    product(gl, kr, lower)

    def right(begin, rows, real, imag):
        out[0, rows, side] = real - far_near[0, rows, side]
        out[1, rows, side] = imag - far_near[1, rows, side]

    product(gl, er, right)


def shadow_kernel(info, mf, nf, near, zr, pf, ml, mr, nl, nr, gl):
    count = zr.shape[1] // 2
    strands = mf.shape[1]
    rows = pl.ds(places(info, count)[0], count)
    head = pl.ds(0, strands)
    pf[...] = mf[...]
    put_left(ml, ALL, mf[0], mf[1])
    put_left(nl, ALL, nf[0], nf[1])
    put_right(nr, 0, ALL, nf[0], nf[1])

    def finish(begin, rows, real, imag):
        pf[0, rows, :] = real
        pf[1, rows, :] = imag

    inverse_tail(pf, ml, mr, nf, nl, nr, finish)
    zr[:, :count, :] = pf[:, rows, :]
    put_right(mr, 0, ALL, pf[0], pf[1])
    put_left(gl, ALL, near[0, rows, head], near[1, rows, head])

    def emit(begin, rows, real, imag):
        zr[0, count:, :] = real
        zr[1, count:, :] = imag

    product(gl, mr, emit)


def coarse_kernel(info, own, other, keep, fine, xf, xr, wr, vr, ml, kl):
    load_step(info, own, other, None, ml, None)
    count = own.shape[1]
    strands = keep.shape[2]
    for start, source in zip(places(info, count), (own, other)):
        xf[:, pl.ds(start, count), :] = source[:, :, strands:]
    put_left(kl, ALL, keep[0], keep[1])
    real, imag = xf[0], xf[1]
    for _ in range(7):
        real, imag = apply(ml, real, imag)
        real = xf[0] + real
        imag = xf[1] + imag
    real = 0.2 * real
    imag = 0.2 * imag
    xf[0] = real
    xf[1] = imag
    xr[...] = xf[:, pl.ds(places(info, count)[0], count), :]
    real, imag = apply(kl, real, imag)
    wr[0] = real
    wr[1] = imag
    vr[0] = fine[0, :, strands:] + real
    vr[1] = fine[1, :, strands:] + imag


def side_kernel(info, near, far, xf, odd, fl):
    count = odd.shape[1]
    strands = far.shape[2]
    rows = pl.ds(places(info, count)[0], count)
    put_left(fl, ALL, far[0, rows, :], far[1, rows, :])
    real, imag = apply(fl, xf[0], xf[1])
    odd[0] = near[0, rows, strands:] - real
    odd[1] = near[1, rows, strands:] - imag


def last_kernel(info, own, other, zr, base, middle, odd, zl, vf):
    count = own.shape[1]
    for start, source in zip(places(info, count), (own, other)):
        vf[:, pl.ds(start, count), :] = source[...]
    put_left(zl, ALL, zr[0], zr[1])
    real, imag = apply(zl, vf[0], vf[1])
    middle[0] = real[:count]
    middle[1] = imag[:count]
    odd[0] = base[0] - real[count:]
    odd[1] = base[1] - imag[count:]


VMEM = pl.BlockSpec(memory_space=pltpu.VMEM)
SMEM = pl.BlockSpec(memory_space=pltpu.SMEM)


def size(shape, dtype):
    total = jnp.dtype(dtype).itemsize
    for extent in shape:
        total *= extent
    return total


def call(kernel, info, arrays, outs, scratch, flops):
    shapes = [jax.ShapeDtypeStruct(shape, F32) for shape in outs]
    moved = sum(size(x.shape, x.dtype) for x in list(arrays) + shapes)
    held = sum(size(*item) for item in scratch)
    return pl.pallas_call(
        kernel,
        out_shape=shapes,
        in_specs=[SMEM] + [VMEM] * len(arrays),
        out_specs=[VMEM] * len(outs),
        scratch_shapes=[pltpu.VMEM(*item) for item in scratch],
        compiler_params=pltpu.CompilerParams(
            vmem_limit_bytes=min(60 * 2**20, moved + held + 16 * 2**20)
        ),
        cost_estimate=pl.CostEstimate(
            flops=int(flops) // SHARE, bytes_accessed=int(moved) // SHARE, transcendentals=0
        ),
    )(info, *arrays)


def body(diag_block, lower_block, upper_block, twist, excitation):
    slabs = lax.axis_size("slab")
    slab = lax.axis_index("slab")
    row = lax.axis_index("row")
    diag, lower, upper, drive = diag_block[0], lower_block[0], upper_block[0], excitation[0]
    count, strands = diag.shape[1:]
    width = drive.shape[2]
    narrow = strands + width
    wide = strands + narrow
    info = jnp.stack([row, (slab % 4 == 1).astype(row.dtype)]).astype(jnp.int32)
    unit = 18 * strands**3

    def pairs(phase, by):
        return [
            (i, i + by) for i in range(slabs) if i % 4 == phase and 0 <= i + by < slabs
        ]

    def send(x, *moves):
        return lax.ppermute(x, "slab", [pair for move in moves for pair in pairs(*move)])

    def cross(x):
        return lax.ppermute(x, "row", [(0, 1), (1, 0)])

    def after(x, *gates):
        return lax.optimization_barrier((x,) + gates)[0]

    part = (2, count, strands)
    part_narrow = (2, count, narrow)
    part_thin = (2, count, width)
    full = (2, strands, strands)
    left = ((3, strands, 3 * strands), BF16)
    left_half = ((3, count, 3 * strands), BF16)

    def right(columns):
        return ((3, 3 * strands, columns), BF16)

    marks = jnp.broadcast_to(twist.astype(F32), (2, MARK, strands))
    below_rows = jnp.concatenate([upper, marks], axis=1)
    above_rows = jnp.concatenate([lower, marks], axis=1)
    below = send(below_rows, (2, 1), (0, 1))
    above = send(above_rows, (2, -1), (0, -1))
    diag_other = cross(diag)
    lower, upper, drive = lax.optimization_barrier(
        (lower, upper, drive, below_rows, above_rows)
    )[:3]
    joined = jnp.concatenate([lower, drive, upper], axis=2)
    joined_other = cross(joined)
    base = jnp.concatenate([diag, drive], axis=2)
    base_swap = send(base, (2, -2), (0, 2))
    near, far = call(
        first_kernel, info, [diag, diag_other, joined, joined_other, twist],
        [(2, strands, narrow), full],
        [(full, F32), left, right(strands)] * 2 + [right(wide)],
        unit * 6.5,
    )
    is_q = slab % 4 == 0
    base_swap = after(base_swap, near)
    base_pay = jnp.where(is_q, base_swap, base)
    base_fine = send(base_pay, (2, 1), (0, 1))
    near, base_pay = lax.optimization_barrier((near, base_pay))
    pick = ((strands, strands), BF16)
    pieces = [above, below]
    (sent,) = call(
        keep_kernel, info, pieces + [near],
        [part_narrow], [left_half, right(narrow), pick], unit * 0.625,
    )
    got = send(sent, (1, 2), (3, -2))
    (keep,) = call(
        keep_kernel, info, pieces + [after(far, sent)],
        [part], [left_half, right(strands), pick], unit * 0.5,
    )
    keep_other = cross(keep)
    far_near, far_far = call(
        outer_kernel, info, pieces + [near, after(far, keep)],
        [part_narrow, part], [left_half, right(narrow), right(strands), pick], unit * 1.125,
    )
    fine = base_fine - after(sent, far_near) - got
    base_coarse = send(
        after(jnp.where(is_q, base, base_swap), fine), (2, -3), (0, 1)
    )
    fine_other = cross(fine)
    out, mf, nf = call(
        second_kernel, info,
        [fine, fine_other, keep, keep_other, far_near, far_far],
        [part_narrow, full, full],
        [left, right(strands), right(strands), left_half, right(strands), right(width)]
        + [(part, F32)] * 2,
        unit * 3.625,
    )
    out_got = send(out, (3, 2), (1, -2))
    (zr,) = call(
        shadow_kernel, info, [mf, nf, near], [full],
        [(full, F32), left, right(strands), left, right(strands), left_half], unit * 3.5,
    )
    total = after(out, zr) + base_coarse + out_got
    total_other = cross(total)
    left_two = ((2, strands, 3 * strands), BF16)
    xf, xr, wr, vr = call(
        coarse_kernel, info, [total, total_other, keep, fine],
        [(2, strands, width), part_thin, part_thin, part_thin],
        [left_two, ((2, count, 3 * strands), BF16)], unit * 2.5,
    )
    w_got = send(wr, (1, 2), (3, -2))
    x_even = send(xr, (1, -1))
    (base_odd,) = call(
        side_kernel, info, [near, far, xf], [part_thin],
        [((2, count, 3 * strands), BF16)], unit * 0.2,
    )
    v = after(vr, base_odd) + w_got
    v_other = cross(v)
    middle, odd = call(
        last_kernel, info, [v, v_other, zr, base_odd], [part_thin, part_thin],
        [left_two, ((2, strands, width), F32)], unit * 0.5,
    )
    x_middle = send(middle, (3, -1))
    return jnp.where(slab % 2 == 1, odd, x_even + x_middle)[None]


def solution(mesh):
    return jax.shard_map(
        body,
        mesh=mesh,
        in_specs=(
            P("slab", None, "row", None),
            P("slab", None, "row", None),
            P("slab", None, "row", None),
            P("slab", None),
            P("slab", None, "row", None),
        ),
        out_specs=P("slab", None, "row", None),
        check_vma=False,
    )
```

```python
import jax
import jax.numpy as jnp
from jax import lax
from jax.experimental import pallas as pl
from jax.experimental.pallas import tpu as pltpu
from jax.sharding import PartitionSpec as P

F32 = jnp.float32
BF16 = jnp.bfloat16
ALL = slice(None)
TILE = 256
MARK = 8
SHARE = 4096


def halves(x):
    high = x.astype(BF16)
    return high, (x - high.astype(F32)).astype(BF16)


def dot(a, b):
    return jnp.dot(a, b, preferred_element_type=F32)


def put_left(ref, rows, real, imag):
    depth = ref.shape[2] // 3
    spans = [pl.ds(block * depth, depth) for block in range(3)]
    for part, value in enumerate((real, imag, real + imag)[: ref.shape[0]]):
        high, low = halves(value)
        ref[part, rows, spans[0]] = high
        ref[part, rows, spans[1]] = low
        ref[part, rows, spans[2]] = high


def put_right(ref, start, cols, real, imag):
    depth = ref.shape[1] // 3
    count = real.shape[0]
    spans = [pl.ds(pl.multiple_of(block * depth + start, 128), count) for block in range(3)]
    for part, value in enumerate((real, imag, real + imag)):
        high, low = halves(value)
        ref[part, spans[0], cols] = high
        ref[part, spans[1], cols] = high
        ref[part, spans[2], cols] = low


def product(left, right, emit, start=0, width=None):
    width = right.shape[2] if width is None else width
    count = left.shape[1]
    cols = pl.ds(start, width)

    def step(begin, extent):
        rows = pl.ds(begin, extent)
        first = dot(left[0, rows, :], right[0, :, cols])
        second = dot(left[1, rows, :], right[1, :, cols])
        third = dot(left[2, rows, :], right[2, :, cols])
        emit(begin, rows, first - second, third - first - second)

    if count <= TILE:
        step(0, count)
    else:

        @pl.loop(0, count // TILE)
        def _(index):
            step(pl.multiple_of(index * TILE, TILE), TILE)


def fill(target):
    def emit(begin, rows, real, imag):
        target[0, rows, :] = real
        target[1, rows, :] = imag

    return emit


def apply(left, real, imag, rows=ALL):
    width = real.shape[1]
    high, low = halves(jnp.concatenate([real, imag], axis=1))
    stacked = jnp.concatenate([high, high, low], axis=0)
    first = dot(left[0, rows, :], stacked)
    second = dot(left[1, rows, :], stacked)
    return (
        first[:, :width] - second[:, width:],
        first[:, width:] + second[:, :width],
    )


def eye(rows, cols, row_start):
    return (
        lax.broadcasted_iota(jnp.int32, (rows, cols), 0) + row_start
        == lax.broadcasted_iota(jnp.int32, (rows, cols), 1)
    ).astype(F32)


def places(info, count):
    return (
        pl.multiple_of(info[0] * count, count),
        pl.multiple_of((1 - info[0]) * count, count),
    )


def one_hot(order):
    strands = order.shape[1]
    return (lax.broadcasted_iota(jnp.int32, (strands, strands), 0) == order).astype(BF16)


def twisted(real, imag, pick):
    count = real.shape[0]
    moved = dot(jnp.concatenate(halves(real) + halves(imag), axis=0), pick)
    return (
        moved[:count] + moved[count : 2 * count],
        moved[2 * count : 3 * count] + moved[3 * count :],
    )


def load_step(info, own, other, mf, left, right):
    count = own.shape[1]
    strands = own.shape[1] * 2
    for start, source in zip(places(info, count), (own, other)):
        rows = pl.ds(start, count)
        real = eye(count, strands, start) - 0.2 * source[0, :, :strands]
        imag = -0.2 * source[1, :, :strands]
        if mf is not None:
            mf[0, rows, :] = real
            mf[1, rows, :] = imag
        put_left(left, rows, real, imag)
        if right is not None:
            put_right(right, start, ALL, real, imag)


def square(ml, mr, nf, nl, nr):
    def emit(begin, rows, real, imag):
        nf[0, rows, :] = real
        nf[1, rows, :] = imag
        if nl is not None:
            put_left(nl, rows, real, imag)
        put_right(nr, begin, ALL, real, imag)

    product(ml, mr, emit)


def inverse_tail(mf, ml, mr, nf, nl, nr, finish):
    strands = mf.shape[1]

    def quarter(begin, rows, real, imag):
        mf[0, rows, :] = (
            mf[0, rows, :] + nf[0, rows, :] + real + eye(real.shape[0], strands, begin)
        )
        mf[1, rows, :] = mf[1, rows, :] + nf[1, rows, :] + imag
        put_right(mr, begin, ALL, mf[0, rows, :], mf[1, rows, :])

    product(ml, nr, quarter)

    def fourth(begin, rows, real, imag):
        put_left(ml, rows, real, imag)

    product(nl, nr, fourth)

    def last(begin, rows, real, imag):
        finish(
            begin, rows, 0.2 * (mf[0, rows, :] + real), 0.2 * (mf[1, rows, :] + imag)
        )

    product(ml, mr, last)


def pack_kernel(order, lower, upper, diag, drive, below, above, joined, base):
    count, strands = lower.shape[1:]
    width = drive.shape[2]
    marks = jnp.broadcast_to(order[...].astype(F32), (MARK, strands))
    below[0, :count, :] = upper[0]
    below[0, count:, :] = marks
    above[0, :count, :] = lower[0]
    above[0, count:, :] = marks
    joined[0, :, :strands] = lower[0]
    joined[0, :, strands : strands + width] = drive[0]
    joined[0, :, strands + width :] = upper[0]
    base[0, :, :strands] = diag[0]
    base[0, :, strands:] = drive[0]


def first_kernel(
    info, own, other, wide_own, wide_other, order, near, far, mf, ml, mr, nf, nl, nr, wr
):
    load_step(info, own, other, mf, ml, mr)
    count = own.shape[1]
    strands = mf.shape[1]
    width = wide_own.shape[2] - 2 * strands
    narrow = strands + width
    is_a = info[1] == 1
    pick = one_hot(order[...])
    low = pl.ds(0, strands)
    side = pl.ds(strands, width)
    up = pl.ds(narrow, strands)
    for start, source in zip(places(info, count), (wide_own, wide_other)):
        put_right(wr, start, side, source[0, :, side], source[1, :, side])
        for cols, swap in ((low, is_a), (up, jnp.logical_not(is_a))):
            real, imag = twisted(
                jnp.where(swap, source[0, :, up], source[0, :, low]),
                jnp.where(swap, source[1, :, up], source[1, :, low]),
                pick,
            )
            put_right(wr, start, cols, real, imag)
    square(ml, mr, nf, nl, nr)

    def finish(begin, rows, real, imag):
        put_left(nl, rows, real, imag)

    inverse_tail(mf, ml, mr, nf, nl, nr, finish)
    product(nl, wr, fill(near), 0, narrow)
    product(nl, wr, fill(far), narrow, strands)


def load_coupling(cl, above, below, swap, pick):
    count = cl.shape[1]
    rows = pl.ds(0, count)
    order = jnp.where(
        swap, above[0, count : count + 1, :], below[0, count : count + 1, :]
    )
    pick[...] = one_hot(order.astype(jnp.int32))
    real, imag = (
        jnp.where(swap, above[part, rows, :], below[part, rows, :]) for part in range(2)
    )
    real, imag = twisted(real, imag, pick[...])
    put_left(cl, ALL, real, imag)


def keep_kernel(info, above, below, far, out, cl, rr, pick):
    load_coupling(cl, above, below, info[1] == 1, pick)
    put_right(rr, 0, ALL, far[0], far[1])
    product(cl, rr, fill(out))


def outer_kernel(
    info, above, below, near, far, near_out, far_out, cl, nr, fr, pick
):
    load_coupling(cl, above, below, info[1] == 0, pick)
    put_right(nr, 0, ALL, near[0], near[1])
    put_right(fr, 0, ALL, far[0], far[1])
    product(cl, nr, fill(near_out))
    product(cl, fr, fill(far_out))


def step_right(source, gl, right, target, base):
    put_left(gl, ALL, source[0], source[1])

    def emit(begin, rows, real, imag):
        target[0, rows, :] = real if base is None else base[0, rows, :] + real
        target[1, rows, :] = imag if base is None else base[1, rows, :] + imag

    product(gl, right, emit)


def second_kernel(
    info, own, other, kc_own, kc_other, far_near, far_far, out, mf, nf,
    ml, mr, nr, gl, kr, er, g, k,
):
    load_step(info, own, other, mf, ml, mr)
    count = own.shape[1]
    strands = mf.shape[1]
    side = pl.ds(strands, own.shape[2] - strands)
    for start, source, edge in zip(places(info, count), (kc_own, kc_other), (own, other)):
        put_right(kr, start, ALL, source[0], source[1])
        put_right(er, start, ALL, edge[0, :, side], edge[1, :, side])
    square(ml, mr, nf, None, nr)
    g[...] = far_near[:, :, :strands]
    step_right(g, gl, mr, k, g)
    step_right(k, gl, nr, g, k)
    step_right(g, gl, nr, k, None)
    step_right(k, gl, nr, k, g)
    put_left(gl, ALL, 0.2 * k[0], 0.2 * k[1])

    head = pl.ds(0, strands)

    def lower(begin, rows, real, imag):
        out[0, rows, head] = -far_far[0, rows, :] - real
        out[1, rows, head] = -far_far[1, rows, :] - imag

    product(gl, kr, lower)

    def right(begin, rows, real, imag):
        out[0, rows, side] = real - far_near[0, rows, side]
        out[1, rows, side] = imag - far_near[1, rows, side]

    product(gl, er, right)


def shadow_kernel(info, mf, nf, near, zr, pf, ml, mr, nl, nr, gl):
    count = zr.shape[1] // 2
    strands = mf.shape[1]
    rows = pl.ds(places(info, count)[0], count)
    head = pl.ds(0, strands)
    pf[...] = mf[...]
    put_left(ml, ALL, mf[0], mf[1])
    put_left(nl, ALL, nf[0], nf[1])
    put_right(nr, 0, ALL, nf[0], nf[1])

    def finish(begin, rows, real, imag):
        pf[0, rows, :] = real
        pf[1, rows, :] = imag

    inverse_tail(pf, ml, mr, nf, nl, nr, finish)
    zr[:, :count, :] = pf[:, rows, :]
    put_right(mr, 0, ALL, pf[0], pf[1])
    put_left(gl, ALL, near[0, rows, head], near[1, rows, head])

    def emit(begin, rows, real, imag):
        zr[0, count:, :] = real
        zr[1, count:, :] = imag

    product(gl, mr, emit)


def coarse_kernel(info, own, other, keep, fine, xf, xr, wr, vr, ml, kl):
    load_step(info, own, other, None, ml, None)
    count = own.shape[1]
    strands = keep.shape[2]
    for start, source in zip(places(info, count), (own, other)):
        xf[:, pl.ds(start, count), :] = source[:, :, strands:]
    put_left(kl, ALL, keep[0], keep[1])
    real, imag = xf[0], xf[1]
    for _ in range(7):
        real, imag = apply(ml, real, imag)
        real = xf[0] + real
        imag = xf[1] + imag
    real = 0.2 * real
    imag = 0.2 * imag
    xf[0] = real
    xf[1] = imag
    xr[...] = xf[:, pl.ds(places(info, count)[0], count), :]
    real, imag = apply(kl, real, imag)
    wr[0] = real
    wr[1] = imag
    vr[0] = fine[0, :, strands:] + real
    vr[1] = fine[1, :, strands:] + imag


def side_kernel(info, near, far, xf, odd, fl):
    count = odd.shape[1]
    strands = far.shape[2]
    rows = pl.ds(places(info, count)[0], count)
    put_left(fl, ALL, far[0, rows, :], far[1, rows, :])
    real, imag = apply(fl, xf[0], xf[1])
    odd[0] = near[0, rows, strands:] - real
    odd[1] = near[1, rows, strands:] - imag


def last_kernel(info, own, other, zr, base, middle, odd, zl, vf):
    count = own.shape[1]
    for start, source in zip(places(info, count), (own, other)):
        vf[:, pl.ds(start, count), :] = source[...]
    put_left(zl, ALL, zr[0], zr[1])
    real, imag = apply(zl, vf[0], vf[1])
    middle[0] = real[:count]
    middle[1] = imag[:count]
    odd[0] = base[0] - real[count:]
    odd[1] = base[1] - imag[count:]


VMEM = pl.BlockSpec(memory_space=pltpu.VMEM)
SMEM = pl.BlockSpec(memory_space=pltpu.SMEM)


def size(shape, dtype):
    total = jnp.dtype(dtype).itemsize
    for extent in shape:
        total *= extent
    return total


def call(kernel, info, arrays, outs, scratch, flops):
    shapes = [jax.ShapeDtypeStruct(shape, F32) for shape in outs]
    moved = sum(size(x.shape, x.dtype) for x in list(arrays) + shapes)
    held = sum(size(*item) for item in scratch)
    return pl.pallas_call(
        kernel,
        out_shape=shapes,
        in_specs=[SMEM] + [VMEM] * len(arrays),
        out_specs=[VMEM] * len(outs),
        scratch_shapes=[pltpu.VMEM(*item) for item in scratch],
        compiler_params=pltpu.CompilerParams(
            vmem_limit_bytes=min(60 * 2**20, moved + held + 16 * 2**20)
        ),
        cost_estimate=pl.CostEstimate(
            flops=int(flops) // SHARE, bytes_accessed=int(moved) // SHARE, transcendentals=0
        ),
    )(info, *arrays)


def body(diag_block, lower_block, upper_block, twist, excitation):
    slabs = lax.axis_size("slab")
    slab = lax.axis_index("slab")
    row = lax.axis_index("row")
    diag, lower, upper, drive = diag_block[0], lower_block[0], upper_block[0], excitation[0]
    count, strands = diag.shape[1:]
    width = drive.shape[2]
    narrow = strands + width
    wide = strands + narrow
    info = jnp.stack([row, (slab % 4 == 1).astype(row.dtype)]).astype(jnp.int32)
    unit = 18 * strands**3

    def pairs(phase, by):
        return [
            (i, i + by) for i in range(slabs) if i % 4 == phase and 0 <= i + by < slabs
        ]

    def send(x, *moves):
        return lax.ppermute(x, "slab", [pair for move in moves for pair in pairs(*move)])

    def cross(x):
        return lax.ppermute(x, "row", [(0, 1), (1, 0)])

    def after(x, *gates):
        return lax.optimization_barrier((x,) + gates)[0]

    part = (2, count, strands)
    part_narrow = (2, count, narrow)
    part_thin = (2, count, width)
    full = (2, strands, strands)
    left = ((3, strands, 3 * strands), BF16)
    left_half = ((3, count, 3 * strands), BF16)

    def right(columns):
        return ((3, 3 * strands, columns), BF16)

    def slice_of(rows, columns):
        return pl.BlockSpec((1, rows, columns), lambda index: (index, 0, 0))

    shapes = [
        (count + MARK, strands), (count + MARK, strands), (count, wide), (count, narrow)
    ]
    below_rows, above_rows, joined, base = pl.pallas_call(
        pack_kernel,
        grid=(2,),
        out_shape=[jax.ShapeDtypeStruct((2, *shape), F32) for shape in shapes],
        in_specs=[pl.BlockSpec((1, strands), lambda index: (0, 0))]
        + [slice_of(count, strands)] * 3 + [slice_of(count, width)],
        out_specs=[slice_of(*shape) for shape in shapes],
        compiler_params=pltpu.CompilerParams(vmem_limit_bytes=60 * 2**20),
    )(twist, lower, upper, diag, drive)
    below = send(below_rows, (2, 1), (0, 1))
    above = send(above_rows, (2, -1), (0, -1))
    diag_other = cross(diag)
    joined_other = cross(joined)
    base_swap = send(base, (2, -2), (0, 2))
    near, far = call(
        first_kernel, info, [diag, diag_other, joined, joined_other, twist],
        [(2, strands, narrow), full],
        [(full, F32), left, right(strands)] * 2 + [right(wide)],
        unit * 6.5,
    )
    is_q = slab % 4 == 0
    base_swap = after(base_swap, near)
    base_pay = jnp.where(is_q, base_swap, base)
    base_fine = send(base_pay, (2, 1), (0, 1))
    near, base_pay = lax.optimization_barrier((near, base_pay))
    pick = ((strands, strands), BF16)
    pieces = [above, below]
    (sent,) = call(
        keep_kernel, info, pieces + [near],
        [part_narrow], [left_half, right(narrow), pick], unit * 0.625,
    )
    got = send(sent, (1, 2), (3, -2))
    (keep,) = call(
        keep_kernel, info, pieces + [after(far, sent)],
        [part], [left_half, right(strands), pick], unit * 0.5,
    )
    keep_other = cross(keep)
    far_near, far_far = call(
        outer_kernel, info, pieces + [near, after(far, keep)],
        [part_narrow, part], [left_half, right(narrow), right(strands), pick], unit * 1.125,
    )
    fine = base_fine - after(sent, far_near) - got
    base_coarse = send(
        after(jnp.where(is_q, base, base_swap), fine), (2, -3), (0, 1)
    )
    fine_other = cross(fine)
    out, mf, nf = call(
        second_kernel, info,
        [fine, fine_other, keep, keep_other, far_near, far_far],
        [part_narrow, full, full],
        [left, right(strands), right(strands), left_half, right(strands), right(width)]
        + [(part, F32)] * 2,
        unit * 3.625,
    )
    out_got = send(out, (3, 2), (1, -2))
    (zr,) = call(
        shadow_kernel, info, [mf, nf, near], [full],
        [(full, F32), left, right(strands), left, right(strands), left_half], unit * 3.5,
    )
    total = after(out, zr) + base_coarse + out_got
    total_other = cross(total)
    left_two = ((2, strands, 3 * strands), BF16)
    xf, xr, wr, vr = call(
        coarse_kernel, info, [total, total_other, keep, fine],
        [(2, strands, width), part_thin, part_thin, part_thin],
        [left_two, ((2, count, 3 * strands), BF16)], unit * 2.5,
    )
    w_got = send(wr, (1, 2), (3, -2))
    x_even = send(xr, (1, -1))
    (base_odd,) = call(
        side_kernel, info, [near, far, xf], [part_thin],
        [((2, count, 3 * strands), BF16)], unit * 0.2,
    )
    v = after(vr, base_odd) + w_got
    v_other = cross(v)
    middle, odd = call(
        last_kernel, info, [v, v_other, zr, base_odd], [part_thin, part_thin],
        [left_two, ((2, strands, width), F32)], unit * 0.5,
    )
    x_middle = send(middle, (3, -1))
    return jnp.where(slab % 2 == 1, odd, x_even + x_middle)[None]


def solution(mesh):
    return jax.shard_map(
        body,
        mesh=mesh,
        in_specs=(
            P("slab", None, "row", None),
            P("slab", None, "row", None),
            P("slab", None, "row", None),
            P("slab", None),
            P("slab", None, "row", None),
        ),
        out_specs=P("slab", None, "row", None),
        check_vma=False,
    )
```

```python
import jax
import jax.numpy as jnp
from jax import lax
from jax.experimental import pallas as pl
from jax.experimental.pallas import tpu as pltpu
from jax.sharding import PartitionSpec as P

F32 = jnp.float32
BF16 = jnp.bfloat16
ALL = slice(None)
TILE = 256
MARK = 8
SHARE = 4096


def halves(x):
    high = x.astype(BF16)
    return high, (x - high.astype(F32)).astype(BF16)


def dot(a, b):
    return jnp.dot(a, b, preferred_element_type=F32)


def put_left(ref, rows, real, imag):
    depth = ref.shape[2] // 3
    spans = [pl.ds(block * depth, depth) for block in range(3)]
    for part, value in enumerate((real, imag, real + imag)[: ref.shape[0]]):
        high, low = halves(value)
        ref[part, rows, spans[0]] = high
        ref[part, rows, spans[1]] = low
        ref[part, rows, spans[2]] = high


def put_right(ref, start, cols, real, imag):
    depth = ref.shape[1] // 3
    count = real.shape[0]
    spans = [pl.ds(pl.multiple_of(block * depth + start, 128), count) for block in range(3)]
    for part, value in enumerate((real, imag, real + imag)):
        high, low = halves(value)
        ref[part, spans[0], cols] = high
        ref[part, spans[1], cols] = high
        ref[part, spans[2], cols] = low


def product(left, right, emit, start=0, width=None):
    width = right.shape[2] if width is None else width
    count = left.shape[1]
    cols = pl.ds(start, width)

    def step(begin, extent):
        rows = pl.ds(begin, extent)
        first = dot(left[0, rows, :], right[0, :, cols])
        second = dot(left[1, rows, :], right[1, :, cols])
        third = dot(left[2, rows, :], right[2, :, cols])
        emit(begin, rows, first - second, third - first - second)

    if count <= TILE:
        step(0, count)
    else:

        @pl.loop(0, count // TILE)
        def _(index):
            step(pl.multiple_of(index * TILE, TILE), TILE)


def fill(target):
    def emit(begin, rows, real, imag):
        target[0, rows, :] = real
        target[1, rows, :] = imag

    return emit


def apply(left, real, imag, rows=ALL):
    width = real.shape[1]
    high, low = halves(jnp.concatenate([real, imag], axis=1))
    stacked = jnp.concatenate([high, high, low], axis=0)
    first = dot(left[0, rows, :], stacked)
    second = dot(left[1, rows, :], stacked)
    return (
        first[:, :width] - second[:, width:],
        first[:, width:] + second[:, :width],
    )


def eye(rows, cols, row_start):
    return (
        lax.broadcasted_iota(jnp.int32, (rows, cols), 0) + row_start
        == lax.broadcasted_iota(jnp.int32, (rows, cols), 1)
    ).astype(F32)


def places(info, count):
    return (
        pl.multiple_of(info[0] * count, count),
        pl.multiple_of((1 - info[0]) * count, count),
    )


def one_hot(order):
    strands = order.shape[1]
    return (lax.broadcasted_iota(jnp.int32, (strands, strands), 0) == order).astype(BF16)


def twisted(real, imag, pick):
    count = real.shape[0]
    moved = dot(jnp.concatenate(halves(real) + halves(imag), axis=0), pick)
    return (
        moved[:count] + moved[count : 2 * count],
        moved[2 * count : 3 * count] + moved[3 * count :],
    )


def load_step(info, own, other, mf, left, right):
    count = own.shape[1]
    strands = own.shape[1] * 2
    for start, source in zip(places(info, count), (own, other)):
        rows = pl.ds(start, count)
        real = eye(count, strands, start) - 0.2 * source[0, :, :strands]
        imag = -0.2 * source[1, :, :strands]
        if mf is not None:
            mf[0, rows, :] = real
            mf[1, rows, :] = imag
        put_left(left, rows, real, imag)
        if right is not None:
            put_right(right, start, ALL, real, imag)


def square(ml, mr, nf, nl, nr):
    def emit(begin, rows, real, imag):
        nf[0, rows, :] = real
        nf[1, rows, :] = imag
        if nl is not None:
            put_left(nl, rows, real, imag)
        put_right(nr, begin, ALL, real, imag)

    product(ml, mr, emit)


def inverse_tail(mf, ml, mr, nf, nl, nr, finish):
    strands = mf.shape[1]

    def quarter(begin, rows, real, imag):
        mf[0, rows, :] = (
            mf[0, rows, :] + nf[0, rows, :] + real + eye(real.shape[0], strands, begin)
        )
        mf[1, rows, :] = mf[1, rows, :] + nf[1, rows, :] + imag
        put_right(mr, begin, ALL, mf[0, rows, :], mf[1, rows, :])

    product(ml, nr, quarter)

    def fourth(begin, rows, real, imag):
        put_left(ml, rows, real, imag)

    product(nl, nr, fourth)

    def last(begin, rows, real, imag):
        finish(
            begin, rows, 0.2 * (mf[0, rows, :] + real), 0.2 * (mf[1, rows, :] + imag)
        )

    product(ml, mr, last)


def pack_kernel(order, lower, upper, diag, drive, below, above, joined, base):
    count, strands = lower.shape[1:]
    width = drive.shape[2]
    marks = jnp.broadcast_to(order[...].astype(F32), (MARK, strands))
    below[0, :count, :] = upper[0]
    below[0, count:, :] = marks
    above[0, :count, :] = lower[0]
    above[0, count:, :] = marks
    joined[0, :, :strands] = lower[0]
    joined[0, :, strands : strands + width] = drive[0]
    joined[0, :, strands + width :] = upper[0]
    base[0, :, :strands] = diag[0]
    base[0, :, strands:] = drive[0]


def first_kernel(
    info, own, other, wide_own, wide_other, order, near, far, mf, ml, mr, nf, nl, nr, wr
):
    load_step(info, own, other, mf, ml, mr)
    count = own.shape[1]
    strands = mf.shape[1]
    width = wide_own.shape[2] - 2 * strands
    narrow = strands + width
    is_a = info[1] == 1
    pick = one_hot(order[...])
    low = pl.ds(0, strands)
    side = pl.ds(strands, width)
    up = pl.ds(narrow, strands)
    for start, source in zip(places(info, count), (wide_own, wide_other)):
        put_right(wr, start, side, source[0, :, side], source[1, :, side])
        for cols, swap in ((low, is_a), (up, jnp.logical_not(is_a))):
            real, imag = twisted(
                jnp.where(swap, source[0, :, up], source[0, :, low]),
                jnp.where(swap, source[1, :, up], source[1, :, low]),
                pick,
            )
            put_right(wr, start, cols, real, imag)
    square(ml, mr, nf, nl, nr)

    def finish(begin, rows, real, imag):
        put_left(nl, rows, real, imag)

    inverse_tail(mf, ml, mr, nf, nl, nr, finish)
    product(nl, wr, fill(near), 0, narrow)
    product(nl, wr, fill(far), narrow, strands)


def load_coupling(cl, above, below, swap, pick):
    count = cl.shape[1]
    rows = pl.ds(0, count)
    order = jnp.where(
        swap, above[0, count : count + 1, :], below[0, count : count + 1, :]
    )
    pick[...] = one_hot(order.astype(jnp.int32))
    real, imag = (
        jnp.where(swap, above[part, rows, :], below[part, rows, :]) for part in range(2)
    )
    real, imag = twisted(real, imag, pick[...])
    put_left(cl, ALL, real, imag)


def keep_kernel(info, above, below, far, out, cl, rr, pick):
    load_coupling(cl, above, below, info[1] == 1, pick)
    put_right(rr, 0, ALL, far[0], far[1])
    product(cl, rr, fill(out))


def outer_kernel(
    info, above, below, near, far, near_out, far_out, cl, nr, fr, pick
):
    load_coupling(cl, above, below, info[1] == 0, pick)
    put_right(nr, 0, ALL, near[0], near[1])
    put_right(fr, 0, ALL, far[0], far[1])
    product(cl, nr, fill(near_out))
    product(cl, fr, fill(far_out))


def step_right(source, gl, right, target, base):
    put_left(gl, ALL, source[0], source[1])

    def emit(begin, rows, real, imag):
        target[0, rows, :] = real if base is None else base[0, rows, :] + real
        target[1, rows, :] = imag if base is None else base[1, rows, :] + imag

    product(gl, right, emit)


def second_kernel(
    info, own, other, kc_own, kc_other, far_near, far_far, out, mf, nf,
    ml, mr, nr, gl, kr, er, g, k,
):
    load_step(info, own, other, mf, ml, mr)
    count = own.shape[1]
    strands = mf.shape[1]
    side = pl.ds(strands, own.shape[2] - strands)
    for start, source, edge in zip(places(info, count), (kc_own, kc_other), (own, other)):
        put_right(kr, start, ALL, source[0], source[1])
        put_right(er, start, ALL, edge[0, :, side], edge[1, :, side])
    square(ml, mr, nf, None, nr)
    g[...] = far_near[:, :, :strands]
    step_right(g, gl, mr, k, g)
    step_right(k, gl, nr, g, k)
    step_right(g, gl, nr, k, None)
    step_right(k, gl, nr, k, g)
    put_left(gl, ALL, 0.2 * k[0], 0.2 * k[1])

    head = pl.ds(0, strands)

    def lower(begin, rows, real, imag):
        out[0, rows, head] = -far_far[0, rows, :] - real
        out[1, rows, head] = -far_far[1, rows, :] - imag

    product(gl, kr, lower)

    def right(begin, rows, real, imag):
        out[0, rows, side] = real - far_near[0, rows, side]
        out[1, rows, side] = imag - far_near[1, rows, side]

    product(gl, er, right)


def shadow_kernel(info, mf, nf, near, zr, pf, ml, mr, nl, nr, gl):
    count = zr.shape[1] // 2
    strands = mf.shape[1]
    rows = pl.ds(places(info, count)[0], count)
    head = pl.ds(0, strands)
    pf[...] = mf[...]
    put_left(ml, ALL, mf[0], mf[1])
    put_left(nl, ALL, nf[0], nf[1])
    put_right(nr, 0, ALL, nf[0], nf[1])

    def finish(begin, rows, real, imag):
        pf[0, rows, :] = real
        pf[1, rows, :] = imag

    inverse_tail(pf, ml, mr, nf, nl, nr, finish)
    zr[:, :count, :] = pf[:, rows, :]
    put_right(mr, 0, ALL, pf[0], pf[1])
    put_left(gl, ALL, near[0, rows, head], near[1, rows, head])

    def emit(begin, rows, real, imag):
        zr[0, count:, :] = real
        zr[1, count:, :] = imag

    product(gl, mr, emit)


def coarse_kernel(info, own, other, keep, fine, xf, xr, wr, vr, ml, kl):
    load_step(info, own, other, None, ml, None)
    count = own.shape[1]
    strands = keep.shape[2]
    for start, source in zip(places(info, count), (own, other)):
        xf[:, pl.ds(start, count), :] = source[:, :, strands:]
    put_left(kl, ALL, keep[0], keep[1])
    real, imag = xf[0], xf[1]
    for _ in range(7):
        real, imag = apply(ml, real, imag)
        real = xf[0] + real
        imag = xf[1] + imag
    real = 0.2 * real
    imag = 0.2 * imag
    xf[0] = real
    xf[1] = imag
    xr[...] = xf[:, pl.ds(places(info, count)[0], count), :]
    real, imag = apply(kl, real, imag)
    wr[0] = real
    wr[1] = imag
    vr[0] = fine[0, :, strands:] + real
    vr[1] = fine[1, :, strands:] + imag


def side_kernel(info, near, far, xf, odd, fl):
    count = odd.shape[1]
    strands = far.shape[2]
    rows = pl.ds(places(info, count)[0], count)
    put_left(fl, ALL, far[0, rows, :], far[1, rows, :])
    real, imag = apply(fl, xf[0], xf[1])
    odd[0] = near[0, rows, strands:] - real
    odd[1] = near[1, rows, strands:] - imag


def last_kernel(info, own, other, zr, base, middle, odd, zl, vf):
    count = own.shape[1]
    for start, source in zip(places(info, count), (own, other)):
        vf[:, pl.ds(start, count), :] = source[...]
    put_left(zl, ALL, zr[0], zr[1])
    real, imag = apply(zl, vf[0], vf[1])
    middle[0] = real[:count]
    middle[1] = imag[:count]
    odd[0] = base[0] - real[count:]
    odd[1] = base[1] - imag[count:]


VMEM = pl.BlockSpec(memory_space=pltpu.VMEM)
SMEM = pl.BlockSpec(memory_space=pltpu.SMEM)


def size(shape, dtype):
    total = jnp.dtype(dtype).itemsize
    for extent in shape:
        total *= extent
    return total


def call(kernel, info, arrays, outs, scratch, flops):
    shapes = [jax.ShapeDtypeStruct(shape, F32) for shape in outs]
    moved = sum(size(x.shape, x.dtype) for x in list(arrays) + shapes)
    held = sum(size(*item) for item in scratch)
    return pl.pallas_call(
        kernel,
        out_shape=shapes,
        in_specs=[SMEM] + [VMEM] * len(arrays),
        out_specs=[VMEM] * len(outs),
        scratch_shapes=[pltpu.VMEM(*item) for item in scratch],
        compiler_params=pltpu.CompilerParams(
            vmem_limit_bytes=min(60 * 2**20, moved + held + 16 * 2**20)
        ),
        cost_estimate=pl.CostEstimate(
            flops=int(flops) // SHARE, bytes_accessed=int(moved) // SHARE, transcendentals=0
        ),
    )(info, *arrays)


def body(diag_block, lower_block, upper_block, twist, excitation):
    slabs = lax.axis_size("slab")
    slab = lax.axis_index("slab")
    row = lax.axis_index("row")
    diag, lower, upper, drive = diag_block[0], lower_block[0], upper_block[0], excitation[0]
    count, strands = diag.shape[1:]
    width = drive.shape[2]
    narrow = strands + width
    wide = strands + narrow
    info = jnp.stack([row, (slab % 4 == 1).astype(row.dtype)]).astype(jnp.int32)
    unit = 18 * strands**3

    def pairs(phase, by):
        return [
            (i, i + by) for i in range(slabs) if i % 4 == phase and 0 <= i + by < slabs
        ]

    def send(x, *moves):
        return lax.ppermute(x, "slab", [pair for move in moves for pair in pairs(*move)])

    def cross(x):
        return lax.ppermute(x, "row", [(0, 1), (1, 0)])

    def after(x, *gates):
        return lax.optimization_barrier((x,) + gates)[0]

    part = (2, count, strands)
    part_narrow = (2, count, narrow)
    part_thin = (2, count, width)
    full = (2, strands, strands)
    left = ((3, strands, 3 * strands), BF16)
    left_half = ((3, count, 3 * strands), BF16)

    def right(columns):
        return ((3, 3 * strands, columns), BF16)

    def slice_of(rows, columns):
        return pl.BlockSpec((1, rows, columns), lambda index: (index, 0, 0))

    shapes = [
        (count + MARK, strands), (count + MARK, strands), (count, wide), (count, narrow)
    ]
    below_rows, above_rows, joined, base = pl.pallas_call(
        pack_kernel,
        grid=(2,),
        out_shape=[jax.ShapeDtypeStruct((2, *shape), F32) for shape in shapes],
        in_specs=[pl.BlockSpec((1, strands), lambda index: (0, 0))]
        + [slice_of(count, strands)] * 3 + [slice_of(count, width)],
        out_specs=[slice_of(*shape) for shape in shapes],
        compiler_params=pltpu.CompilerParams(vmem_limit_bytes=60 * 2**20),
    )(twist, lower, upper, diag, drive)
    below = send(below_rows, (2, 1), (0, 1))
    above = send(above_rows, (2, -1), (0, -1))
    diag_other = cross(diag)
    joined_other = cross(joined)
    base_swap = send(base, (2, -2), (0, 2))
    near, far = call(
        first_kernel, info, [diag, diag_other, joined, joined_other, twist],
        [(2, strands, narrow), full],
        [(full, F32), left, right(strands)] * 2 + [right(wide)],
        unit * 6.5,
    )
    is_q = slab % 4 == 0
    base_swap = after(base_swap, near)
    base_pay = jnp.where(is_q, base_swap, base)
    base_fine = send(base_pay, (2, 1), (0, 1))
    near, base_pay = lax.optimization_barrier((near, base_pay))
    pick = ((strands, strands), BF16)
    pieces = [above, below]
    (sent,) = call(
        keep_kernel, info, pieces + [near],
        [part_narrow], [left_half, right(narrow), pick], unit * 0.625,
    )
    got = send(sent, (1, 2), (3, -2))
    (keep,) = call(
        keep_kernel, info, pieces + [after(far, sent)],
        [part], [left_half, right(strands), pick], unit * 0.5,
    )
    keep_other = cross(keep)
    far_near, far_far = call(
        outer_kernel, info, pieces + [near, after(far, keep)],
        [part_narrow, part], [left_half, right(narrow), right(strands), pick], unit * 1.125,
    )
    fine = base_fine - after(sent, far_near, keep_other) - got
    base_coarse = send(
        after(jnp.where(is_q, base, base_swap), fine), (2, -3), (0, 1)
    )
    fine_other = cross(fine)
    out, mf, nf = call(
        second_kernel, info,
        [fine, fine_other, keep, keep_other, far_near, far_far],
        [part_narrow, full, full],
        [left, right(strands), right(strands), left_half, right(strands), right(width)]
        + [(part, F32)] * 2,
        unit * 3.625,
    )
    out_got = send(out, (3, 2), (1, -2))
    (zr,) = call(
        shadow_kernel, info, [mf, nf, near], [full],
        [(full, F32), left, right(strands), left, right(strands), left_half], unit * 3.5,
    )
    total = after(out, zr) + base_coarse + out_got
    total_other = cross(total)
    left_two = ((2, strands, 3 * strands), BF16)
    xf, xr, wr, vr = call(
        coarse_kernel, info, [total, total_other, keep, fine],
        [(2, strands, width), part_thin, part_thin, part_thin],
        [left_two, ((2, count, 3 * strands), BF16)], unit * 2.5,
    )
    w_got = send(wr, (1, 2), (3, -2))
    x_even = send(xr, (1, -1))
    (base_odd,) = call(
        side_kernel, info, [near, far, xf], [part_thin],
        [((2, count, 3 * strands), BF16)], unit * 0.2,
    )
    v = after(vr, base_odd) + w_got
    v_other = cross(v)
    middle, odd = call(
        last_kernel, info, [v, v_other, zr, base_odd], [part_thin, part_thin],
        [left_two, ((2, strands, width), F32)], unit * 0.5,
    )
    x_middle = send(middle, (3, -1))
    return jnp.where(slab % 2 == 1, odd, x_even + x_middle)[None]


def solution(mesh):
    return jax.shard_map(
        body,
        mesh=mesh,
        in_specs=(
            P("slab", None, "row", None),
            P("slab", None, "row", None),
            P("slab", None, "row", None),
            P("slab", None),
            P("slab", None, "row", None),
        ),
        out_specs=P("slab", None, "row", None),
        check_vma=False,
    )
```

```python
import jax
import jax.numpy as jnp
from jax import lax
from jax.experimental import pallas as pl
from jax.experimental.pallas import tpu as pltpu
from jax.sharding import PartitionSpec as P

F32 = jnp.float32
BF16 = jnp.bfloat16
ALL = slice(None)
TILE = 256
MARK = 8
SHARE = 1


def halves(x):
    high = x.astype(BF16)
    return high, (x - high.astype(F32)).astype(BF16)


def dot(a, b):
    return jnp.dot(a, b, preferred_element_type=F32)


def put_left(ref, rows, real, imag):
    depth = ref.shape[2] // 3
    spans = [pl.ds(block * depth, depth) for block in range(3)]
    for part, value in enumerate((real, imag, real + imag)[: ref.shape[0]]):
        high, low = halves(value)
        ref[part, rows, spans[0]] = high
        ref[part, rows, spans[1]] = low
        ref[part, rows, spans[2]] = high


def put_right(ref, start, cols, real, imag):
    depth = ref.shape[1] // 3
    count = real.shape[0]
    spans = [pl.ds(pl.multiple_of(block * depth + start, 128), count) for block in range(3)]
    for part, value in enumerate((real, imag, real + imag)):
        high, low = halves(value)
        ref[part, spans[0], cols] = high
        ref[part, spans[1], cols] = high
        ref[part, spans[2], cols] = low


def product(left, right, emit, start=0, width=None):
    width = right.shape[2] if width is None else width
    count = left.shape[1]
    cols = pl.ds(start, width)

    def step(begin, extent):
        rows = pl.ds(begin, extent)
        first = dot(left[0, rows, :], right[0, :, cols])
        second = dot(left[1, rows, :], right[1, :, cols])
        third = dot(left[2, rows, :], right[2, :, cols])
        emit(begin, rows, first - second, third - first - second)

    if count <= TILE:
        step(0, count)
    else:

        @pl.loop(0, count // TILE)
        def _(index):
            step(pl.multiple_of(index * TILE, TILE), TILE)


def fill(target):
    def emit(begin, rows, real, imag):
        target[0, rows, :] = real
        target[1, rows, :] = imag

    return emit


def apply(left, real, imag, rows=ALL):
    width = real.shape[1]
    high, low = halves(jnp.concatenate([real, imag], axis=1))
    stacked = jnp.concatenate([high, high, low], axis=0)
    first = dot(left[0, rows, :], stacked)
    second = dot(left[1, rows, :], stacked)
    return (
        first[:, :width] - second[:, width:],
        first[:, width:] + second[:, :width],
    )


def eye(rows, cols, row_start):
    return (
        lax.broadcasted_iota(jnp.int32, (rows, cols), 0) + row_start
        == lax.broadcasted_iota(jnp.int32, (rows, cols), 1)
    ).astype(F32)


def places(info, count):
    return (
        pl.multiple_of(info[0] * count, count),
        pl.multiple_of((1 - info[0]) * count, count),
    )


def one_hot(order):
    strands = order.shape[1]
    return (lax.broadcasted_iota(jnp.int32, (strands, strands), 0) == order).astype(BF16)


def twisted(real, imag, pick):
    count = real.shape[0]
    moved = dot(jnp.concatenate(halves(real) + halves(imag), axis=0), pick)
    return (
        moved[:count] + moved[count : 2 * count],
        moved[2 * count : 3 * count] + moved[3 * count :],
    )


def load_step(info, own, other, mf, left, right):
    count = own.shape[1]
    strands = own.shape[1] * 2
    for start, source in zip(places(info, count), (own, other)):
        rows = pl.ds(start, count)
        real = eye(count, strands, start) - 0.2 * source[0, :, :strands]
        imag = -0.2 * source[1, :, :strands]
        if mf is not None:
            mf[0, rows, :] = real
            mf[1, rows, :] = imag
        put_left(left, rows, real, imag)
        if right is not None:
            put_right(right, start, ALL, real, imag)


def square(ml, mr, nf, nl, nr):
    def emit(begin, rows, real, imag):
        nf[0, rows, :] = real
        nf[1, rows, :] = imag
        if nl is not None:
            put_left(nl, rows, real, imag)
        put_right(nr, begin, ALL, real, imag)

    product(ml, mr, emit)


def inverse_tail(mf, ml, mr, nf, nl, nr, finish):
    strands = mf.shape[1]

    def quarter(begin, rows, real, imag):
        mf[0, rows, :] = (
            mf[0, rows, :] + nf[0, rows, :] + real + eye(real.shape[0], strands, begin)
        )
        mf[1, rows, :] = mf[1, rows, :] + nf[1, rows, :] + imag
        put_right(mr, begin, ALL, mf[0, rows, :], mf[1, rows, :])

    product(ml, nr, quarter)

    def fourth(begin, rows, real, imag):
        put_left(ml, rows, real, imag)

    product(nl, nr, fourth)

    def last(begin, rows, real, imag):
        finish(
            begin, rows, 0.2 * (mf[0, rows, :] + real), 0.2 * (mf[1, rows, :] + imag)
        )

    product(ml, mr, last)


def pack_kernel(order, lower, upper, diag, drive, below, above, joined, base):
    count, strands = lower.shape[1:]
    width = drive.shape[2]
    marks = jnp.broadcast_to(order[...].astype(F32), (MARK, strands))
    below[0, :count, :] = upper[0]
    below[0, count:, :] = marks
    above[0, :count, :] = lower[0]
    above[0, count:, :] = marks
    joined[0, :, :strands] = lower[0]
    joined[0, :, strands : strands + width] = drive[0]
    joined[0, :, strands + width :] = upper[0]
    base[0, :, :strands] = diag[0]
    base[0, :, strands:] = drive[0]


def first_kernel(
    info, own, other, wide_own, wide_other, order, near, far, mf, ml, mr, nf, nl, nr, wr
):
    load_step(info, own, other, mf, ml, mr)
    count = own.shape[1]
    strands = mf.shape[1]
    width = wide_own.shape[2] - 2 * strands
    narrow = strands + width
    is_a = info[1] == 1
    pick = one_hot(order[...])
    low = pl.ds(0, strands)
    side = pl.ds(strands, width)
    up = pl.ds(narrow, strands)
    for start, source in zip(places(info, count), (wide_own, wide_other)):
        put_right(wr, start, side, source[0, :, side], source[1, :, side])
        for cols, swap in ((low, is_a), (up, jnp.logical_not(is_a))):
            real, imag = twisted(
                jnp.where(swap, source[0, :, up], source[0, :, low]),
                jnp.where(swap, source[1, :, up], source[1, :, low]),
                pick,
            )
            put_right(wr, start, cols, real, imag)
    square(ml, mr, nf, nl, nr)

    def finish(begin, rows, real, imag):
        put_left(nl, rows, real, imag)

    inverse_tail(mf, ml, mr, nf, nl, nr, finish)
    product(nl, wr, fill(near), 0, narrow)
    product(nl, wr, fill(far), narrow, strands)


def load_coupling(cl, above, below, swap, pick):
    count = cl.shape[1]
    rows = pl.ds(0, count)
    order = jnp.where(
        swap, above[0, count : count + 1, :], below[0, count : count + 1, :]
    )
    pick[...] = one_hot(order.astype(jnp.int32))
    real, imag = (
        jnp.where(swap, above[part, rows, :], below[part, rows, :]) for part in range(2)
    )
    real, imag = twisted(real, imag, pick[...])
    put_left(cl, ALL, real, imag)


def keep_kernel(info, above, below, far, out, cl, rr, pick):
    load_coupling(cl, above, below, info[1] == 1, pick)
    put_right(rr, 0, ALL, far[0], far[1])
    product(cl, rr, fill(out))


def outer_kernel(
    info, above, below, near, far, near_out, far_out, cl, nr, fr, pick
):
    load_coupling(cl, above, below, info[1] == 0, pick)
    put_right(nr, 0, ALL, near[0], near[1])
    put_right(fr, 0, ALL, far[0], far[1])
    product(cl, nr, fill(near_out))
    product(cl, fr, fill(far_out))


def step_right(source, gl, right, target, base):
    put_left(gl, ALL, source[0], source[1])

    def emit(begin, rows, real, imag):
        target[0, rows, :] = real if base is None else base[0, rows, :] + real
        target[1, rows, :] = imag if base is None else base[1, rows, :] + imag

    product(gl, right, emit)


def second_kernel(
    info, own, other, kc_own, kc_other, far_near, far_far, out, mf, nf,
    ml, mr, nr, gl, kr, er, g, k,
):
    load_step(info, own, other, mf, ml, mr)
    count = own.shape[1]
    strands = mf.shape[1]
    side = pl.ds(strands, own.shape[2] - strands)
    for start, source, edge in zip(places(info, count), (kc_own, kc_other), (own, other)):
        put_right(kr, start, ALL, source[0], source[1])
        put_right(er, start, ALL, edge[0, :, side], edge[1, :, side])
    square(ml, mr, nf, None, nr)
    g[...] = far_near[:, :, :strands]
    step_right(g, gl, mr, k, g)
    step_right(k, gl, nr, g, k)
    step_right(g, gl, nr, k, None)
    step_right(k, gl, nr, k, g)
    put_left(gl, ALL, 0.2 * k[0], 0.2 * k[1])

    head = pl.ds(0, strands)

    def lower(begin, rows, real, imag):
        out[0, rows, head] = -far_far[0, rows, :] - real
        out[1, rows, head] = -far_far[1, rows, :] - imag

    product(gl, kr, lower)

    def right(begin, rows, real, imag):
        out[0, rows, side] = real - far_near[0, rows, side]
        out[1, rows, side] = imag - far_near[1, rows, side]

    product(gl, er, right)


def shadow_kernel(info, mf, nf, near, zr, pf, ml, mr, nl, nr, gl):
    count = zr.shape[1] // 2
    strands = mf.shape[1]
    rows = pl.ds(places(info, count)[0], count)
    head = pl.ds(0, strands)
    pf[...] = mf[...]
    put_left(ml, ALL, mf[0], mf[1])
    put_left(nl, ALL, nf[0], nf[1])
    put_right(nr, 0, ALL, nf[0], nf[1])

    def finish(begin, rows, real, imag):
        pf[0, rows, :] = real
        pf[1, rows, :] = imag

    inverse_tail(pf, ml, mr, nf, nl, nr, finish)
    zr[:, :count, :] = pf[:, rows, :]
    put_right(mr, 0, ALL, pf[0], pf[1])
    put_left(gl, ALL, near[0, rows, head], near[1, rows, head])

    def emit(begin, rows, real, imag):
        zr[0, count:, :] = real
        zr[1, count:, :] = imag

    product(gl, mr, emit)


def coarse_kernel(info, own, other, keep, fine, xf, xr, wr, vr, ml, kl):
    load_step(info, own, other, None, ml, None)
    count = own.shape[1]
    strands = keep.shape[2]
    for start, source in zip(places(info, count), (own, other)):
        xf[:, pl.ds(start, count), :] = source[:, :, strands:]
    put_left(kl, ALL, keep[0], keep[1])
    real, imag = xf[0], xf[1]
    for _ in range(7):
        real, imag = apply(ml, real, imag)
        real = xf[0] + real
        imag = xf[1] + imag
    real = 0.2 * real
    imag = 0.2 * imag
    xf[0] = real
    xf[1] = imag
    xr[...] = xf[:, pl.ds(places(info, count)[0], count), :]
    real, imag = apply(kl, real, imag)
    wr[0] = real
    wr[1] = imag
    vr[0] = fine[0, :, strands:] + real
    vr[1] = fine[1, :, strands:] + imag


def side_kernel(info, near, far, xf, odd, fl):
    count = odd.shape[1]
    strands = far.shape[2]
    rows = pl.ds(places(info, count)[0], count)
    put_left(fl, ALL, far[0, rows, :], far[1, rows, :])
    real, imag = apply(fl, xf[0], xf[1])
    odd[0] = near[0, rows, strands:] - real
    odd[1] = near[1, rows, strands:] - imag


def last_kernel(info, own, other, zr, base, middle, odd, zl, vf):
    count = own.shape[1]
    for start, source in zip(places(info, count), (own, other)):
        vf[:, pl.ds(start, count), :] = source[...]
    put_left(zl, ALL, zr[0], zr[1])
    real, imag = apply(zl, vf[0], vf[1])
    middle[0] = real[:count]
    middle[1] = imag[:count]
    odd[0] = base[0] - real[count:]
    odd[1] = base[1] - imag[count:]


VMEM = pl.BlockSpec(memory_space=pltpu.VMEM)
SMEM = pl.BlockSpec(memory_space=pltpu.SMEM)


def size(shape, dtype):
    total = jnp.dtype(dtype).itemsize
    for extent in shape:
        total *= extent
    return total


def call(kernel, info, arrays, outs, scratch, flops):
    shapes = [jax.ShapeDtypeStruct(shape, F32) for shape in outs]
    moved = sum(size(x.shape, x.dtype) for x in list(arrays) + shapes)
    held = sum(size(*item) for item in scratch)
    return pl.pallas_call(
        kernel,
        out_shape=shapes,
        in_specs=[SMEM] + [VMEM] * len(arrays),
        out_specs=[VMEM] * len(outs),
        scratch_shapes=[pltpu.VMEM(*item) for item in scratch],
        compiler_params=pltpu.CompilerParams(
            vmem_limit_bytes=min(60 * 2**20, moved + held + 16 * 2**20)
        ),
        cost_estimate=pl.CostEstimate(
            flops=int(flops) // SHARE, bytes_accessed=int(moved) // SHARE, transcendentals=0
        ),
    )(info, *arrays)


def body(diag_block, lower_block, upper_block, twist, excitation):
    slabs = lax.axis_size("slab")
    slab = lax.axis_index("slab")
    row = lax.axis_index("row")
    diag, lower, upper, drive = diag_block[0], lower_block[0], upper_block[0], excitation[0]
    count, strands = diag.shape[1:]
    width = drive.shape[2]
    narrow = strands + width
    wide = strands + narrow
    info = jnp.stack([row, (slab % 4 == 1).astype(row.dtype)]).astype(jnp.int32)
    unit = 18 * strands**3

    def pairs(phase, by):
        return [
            (i, i + by) for i in range(slabs) if i % 4 == phase and 0 <= i + by < slabs
        ]

    def send(x, *moves):
        return lax.ppermute(x, "slab", [pair for move in moves for pair in pairs(*move)])

    def cross(x):
        return lax.ppermute(x, "row", [(0, 1), (1, 0)])

    def after(x, *gates):
        return lax.optimization_barrier((x,) + gates)[0]

    part = (2, count, strands)
    part_narrow = (2, count, narrow)
    part_thin = (2, count, width)
    full = (2, strands, strands)
    left = ((3, strands, 3 * strands), BF16)
    left_half = ((3, count, 3 * strands), BF16)

    def right(columns):
        return ((3, 3 * strands, columns), BF16)

    def slice_of(rows, columns):
        return pl.BlockSpec((1, rows, columns), lambda index: (index, 0, 0))

    shapes = [
        (count + MARK, strands), (count + MARK, strands), (count, wide), (count, narrow)
    ]
    below_rows, above_rows, joined, base = pl.pallas_call(
        pack_kernel,
        grid=(2,),
        out_shape=[jax.ShapeDtypeStruct((2, *shape), F32) for shape in shapes],
        in_specs=[pl.BlockSpec((1, strands), lambda index: (0, 0))]
        + [slice_of(count, strands)] * 3 + [slice_of(count, width)],
        out_specs=[slice_of(*shape) for shape in shapes],
        compiler_params=pltpu.CompilerParams(vmem_limit_bytes=60 * 2**20),
    )(twist, lower, upper, diag, drive)
    below = send(below_rows, (2, 1), (0, 1))
    above = send(above_rows, (2, -1), (0, -1))
    diag_other = cross(diag)
    joined_other = cross(joined)
    base_swap = send(base, (2, -2), (0, 2))
    near, far = call(
        first_kernel, info, [diag, diag_other, joined, joined_other, twist],
        [(2, strands, narrow), full],
        [(full, F32), left, right(strands)] * 2 + [right(wide)],
        unit * 6.5,
    )
    is_q = slab % 4 == 0
    base_swap = after(base_swap, near)
    base_pay = jnp.where(is_q, base_swap, base)
    base_fine = send(base_pay, (2, 1), (0, 1))
    near, base_pay = lax.optimization_barrier((near, base_pay))
    pick = ((strands, strands), BF16)
    pieces = [above, below]
    (sent,) = call(
        keep_kernel, info, pieces + [near],
        [part_narrow], [left_half, right(narrow), pick], unit * 0.625,
    )
    got = send(sent, (1, 2), (3, -2))
    (keep,) = call(
        keep_kernel, info, pieces + [after(far, sent)],
        [part], [left_half, right(strands), pick], unit * 0.5,
    )
    keep_other = cross(keep)
    far_near, far_far = call(
        outer_kernel, info, pieces + [near, after(far, keep)],
        [part_narrow, part], [left_half, right(narrow), right(strands), pick], unit * 1.125,
    )
    fine = base_fine - after(sent, far_near, keep_other) - got
    base_coarse = send(
        after(jnp.where(is_q, base, base_swap), fine), (2, -3), (0, 1)
    )
    fine_other = cross(fine)
    out, mf, nf = call(
        second_kernel, info,
        [fine, fine_other, keep, keep_other, far_near, far_far],
        [part_narrow, full, full],
        [left, right(strands), right(strands), left_half, right(strands), right(width)]
        + [(part, F32)] * 2,
        unit * 3.625,
    )
    out_got = send(out, (3, 2), (1, -2))
    (zr,) = call(
        shadow_kernel, info, [mf, nf, near], [full],
        [(full, F32), left, right(strands), left, right(strands), left_half], unit * 3.5,
    )
    total = after(out, zr) + base_coarse + out_got
    total_other = cross(total)
    left_two = ((2, strands, 3 * strands), BF16)
    xf, xr, wr, vr = call(
        coarse_kernel, info, [total, total_other, keep, fine],
        [(2, strands, width), part_thin, part_thin, part_thin],
        [left_two, ((2, count, 3 * strands), BF16)], unit * 2.5,
    )
    w_got = send(wr, (1, 2), (3, -2))
    x_even = send(xr, (1, -1))
    (base_odd,) = call(
        side_kernel, info, [near, far, xf], [part_thin],
        [((2, count, 3 * strands), BF16)], unit * 0.2,
    )
    v = after(vr, base_odd) + w_got
    v_other = cross(v)
    middle, odd = call(
        last_kernel, info, [v, v_other, zr, base_odd], [part_thin, part_thin],
        [left_two, ((2, strands, width), F32)], unit * 0.5,
    )
    x_middle = send(middle, (3, -1))
    return jnp.where(slab % 2 == 1, odd, x_even + x_middle)[None]


def solution(mesh):
    return jax.shard_map(
        body,
        mesh=mesh,
        in_specs=(
            P("slab", None, "row", None),
            P("slab", None, "row", None),
            P("slab", None, "row", None),
            P("slab", None),
            P("slab", None, "row", None),
        ),
        out_specs=P("slab", None, "row", None),
        check_vma=False,
    )
```
